256 devices in a mesh: blk: 8 (over y, x_lo), tr: 32 (over z, x_hi, core).
Axes of the slice: x: 4 (x_hi: 2, x_lo: 2; x = x_hi * 2 + x_lo), y: 4, z: 8, core: 2. Of those that a mesh axis runs over, the one named last changes fastest.
Arguments:
- trial: bfloat16 [8192, 256], P('blk'), may hold values from -6 to 6
- energies: float32 [8192], P(('blk', 'tr')), may hold values from 1 to 3
- kpoint_of: int32 [8192], P('blk'), may hold values from 0 to 15, as said below
- exchange_dens: bfloat16 [8192, 32768], P('blk', 'tr'), may hold values from -0.03125 to 0.03125
- direct_dens: bfloat16 [8192, 4096], P('blk', 'tr'), may hold values from -0.09375 to 0.09375
- coulomb: float32 [32768], P('tr'), may hold values from 0.3 to 3
- screened: bfloat16 [16, 4096, 4096], P('blk', None, 'tr'), may hold values from -0.0234375 to 0.0234375
Outputs:
- applied: float32 [8192, 256], P(('blk', 'tr'))
The draws below stay inside these ranges and needn't reach their ends.
Inputs may be any that keep to these rules, and one draw needn't show every extreme that they name: `kpoint_of`: transition t has a k-point from (t // 1024) * 2 to (t // 1024) * 2 + 1, and every k-point has a transition.
All inputs are finite; a program needn't handle non-finite values.
Results may differ from the reference program's by a relative error of at most 0.0017.
Values may be sent and summed in bfloat16 or wider, within the bound.
A program may use at most 192 MiB of HBM per device.

```python
import math
import jax
import jax.numpy as jnp
from jax import lax

NG = 32768
GW = 4096
NV = 256
KPT = 2
T_GRP = 1024
NK = 16
NT = 8192


def draw_kpoint_of(key, part):
    key = jax.random.fold_in(key, 7)
    position = jnp.arange(NT, dtype=jnp.int32)
    within = position % T_GRP
    base = position // T_GRP * KPT
    random_pick = jax.random.randint(key, (NT,), 0, KPT, dtype=jnp.int32)
    chosen = jnp.where(within < KPT, within, random_pick)
    return (base + chosen).astype(jnp.int32)


def level_of(own_key, dims, split, smallest, largest):
    gain = 1.0
    for axis_at, parts in split:
        draws = jax.random.uniform(jax.random.fold_in(jax.random.fold_in(own_key, 6), axis_at), (parts,), jnp.float32, smallest / len(split), largest / len(split))
        gain = gain * jnp.repeat(jnp.exp(draws), dims[axis_at] // parts).reshape((-1,) + (1,) * (len(dims) - 1 - axis_at))
    return gain


def gaussian(stream_key, shape, deviation, bound, split=(), kind=jnp.bfloat16):
    level = level_of(stream_key, shape, split, -0.22, 0.18) if split else 1.0
    array = jax.random.normal(stream_key, shape, jnp.float32) * deviation * level
    return jnp.minimum(jnp.maximum(array, -bound), bound).astype(kind)


def setup_inputs(seed: int = 0) -> dict:
    seeds = jax.random.split(jax.random.key(seed), 8)
    trial = gaussian(seeds[0], (NT, NV), 1.0, 6.0, ((0, 8),))
    energies = jnp.clip(1.0 + 2.0 * jax.random.uniform(seeds[1], (NT,), jnp.float32) ** level_of(seeds[1], (NT,), ((0, 256),), -0.2, 0.2), 1.0, 3.0)
    kpoint_of = draw_kpoint_of(jax.random.fold_in(seeds[7], 71), 0)
    exchange_dens = gaussian(seeds[3], (NT, NG), NG ** -0.5, 0.03125, ((0, 8), (1, 32)))
    direct_dens = gaussian(seeds[4], (NT, GW), GW ** -0.5, 0.09375, ((0, 8), (1, 32)))
    coulomb = jnp.clip(jnp.exp(math.log(3.0) - 2.3025851 * jax.random.uniform(seeds[5], (NG,), jnp.float32) ** level_of(seeds[5], (NG,), ((0, 32),), -0.2, 0.2)), 0.3, 3.0)
    screened = gaussian(seeds[6], (NK, GW, GW), (GW * NK) ** -0.5, 0.0234375, ((0, 8), (2, 32)))
    return dict(trial=trial, energies=energies, kpoint_of=kpoint_of, exchange_dens=exchange_dens, direct_dens=direct_dens, coulomb=coulomb, screened=screened)


def reference(trial, energies, kpoint_of, exchange_dens, direct_dens, coulomb, screened):
    kpoint_total = screened.shape[0]
    kpoint_ids = jnp.arange(kpoint_total, dtype=jnp.int32)
    belongs = kpoint_of[:, None] == kpoint_ids[None, :]
    weighted = jnp.where(belongs[:, :, None], trial[:, None, :], jnp.zeros((), trial.dtype))
    blocks = jnp.einsum('tg,tkn->kgn', direct_dens.astype(jnp.float32), weighted.astype(jnp.float32)).astype(jnp.bfloat16)

    def accumulate(total, transfer):
        rolled = jnp.take(blocks, (kpoint_ids - transfer) % kpoint_total, axis=0)
        single = lax.dynamic_index_in_dim(screened, transfer, 0, keepdims=False).astype(jnp.float32)
        return total + jnp.einsum('gh,khn->kgn', single, rolled.astype(jnp.float32)), None

    empty = jnp.zeros(blocks.shape, jnp.float32)
    total, unused = lax.scan(accumulate, empty, kpoint_ids)
    potential = total.astype(jnp.bfloat16)
    direct_all = jnp.einsum('tg,kgn->tkn', direct_dens.astype(jnp.float32), potential.astype(jnp.float32))
    direct = jnp.sum(jnp.where(belongs[:, :, None], direct_all, jnp.zeros((), jnp.float32)), axis=1)
    projected = jnp.dot(exchange_dens.T, trial, preferred_element_type=jnp.float32)
    scaled = (coulomb[:, None] * projected).astype(jnp.bfloat16)
    exchange_term = jnp.dot(exchange_dens, scaled, preferred_element_type=jnp.float32)
    return energies[:, None] * trial.astype(jnp.float32) + 2.0 * exchange_term - direct
```

```python
import math

import jax
import jax.numpy as jnp
from jax import lax
from jax.sharding import PartitionSpec as P


def turn(value, angle):
    re, im = value
    c, s = math.cos(angle), math.sin(angle)
    if abs(s) < 1e-9:
        return value
    if abs(c) < 1e-9:
        return (None if im is None else -s * im), s * re
    if im is None:
        return c * re, s * re
    return c * re - s * im, s * re + c * im


def plus(a, b):
    return b if a is None else a if b is None else a + b


def minus(a, b):
    return a if b is None else -b if a is None else a - b


def forward(x):
    n = len(x)
    if n == 1:
        return [(x[0], None)]
    if n == 2:
        return [(x[0] + x[1], None), (x[0] - x[1], None)]
    even, odd = forward(x[0::2]), forward(x[1::2])
    out = [None] * (n // 2 + 1)
    for w in range(n // 4 + 1):
        e, o = even[w], turn(odd[w], -2 * math.pi * w / n)
        out[w] = plus(e[0], o[0]), plus(e[1], o[1])
        if w != n // 2 - w:
            re, im = minus(e[0], o[0]), minus(e[1], o[1])
            out[n // 2 - w] = re, None if im is None else -im
    return out


def backward(y):
    n = 2 * (len(y) - 1)
    if n == 2:
        return [y[0][0] + y[1][0], y[0][0] - y[1][0]]
    even, odd = [], []
    for w in range(n // 4 + 1):
        a, b = y[w], y[n // 2 - w]
        even.append((plus(a[0], b[0]), minus(a[1], b[1])))
        odd.append(turn((minus(a[0], b[0]), plus(a[1], b[1])), 2 * math.pi * w / n))
    for part in (even, odd):
        part[0], part[-1] = (part[0][0], None), (part[-1][0], None)
    out = [None] * n
    out[0::2], out[1::2] = backward(even), backward(odd)
    return out


def per_device(trial, energies, kpoint_of, exchange_dens, direct_dens, coulomb, screened):
    groups, members = lax.axis_size("blk"), lax.axis_size("tr")
    group, member = lax.axis_index("blk"), lax.axis_index("tr")
    kpoints, waves, own_waves = screened.shape
    vectors = trial.shape[1]
    rows = waves // groups // members
    total_k = kpoints * groups
    half = total_k // 2
    f32, bf16 = jnp.float32, jnp.bfloat16

    local = kpoint_of - group * kpoints
    belongs = local[:, None] == jnp.arange(kpoints, dtype=jnp.int32)[None, :]
    masked = jnp.where(belongs[:, :, None], direct_dens[:, None, :], jnp.zeros((), bf16))
    masked = masked.reshape(masked.shape[0], kpoints * own_waves)
    own_blocks = jnp.einsum("tg,tn->gn", masked, trial, preferred_element_type=f32).astype(bf16)
    blocks = lax.all_gather(own_blocks.reshape(kpoints, own_waves, vectors), "blk", axis=0, tiled=True)

    s = screened.reshape(kpoints, members, groups, rows, own_waves)
    s = lax.all_to_all(s, "blk", split_axis=2, concat_axis=0, tiled=True)
    s = s.reshape(total_k, members * rows, own_waves)

    sh = forward([s[q].astype(f32) for q in range(total_k)])
    bh = forward([blocks[q].astype(f32) for q in range(total_k)])
    zero = jnp.zeros((own_waves, vectors), bf16)
    lhs, rhs = [], []
    for w in range(half):
        a, b = (sh[0][0], sh[half][0]) if w == 0 else sh[w]
        c, d = (bh[0][0], bh[half][0]) if w == 0 else bh[w]
        c, d = c.astype(bf16), d.astype(bf16)
        lhs.append(jnp.concatenate([a.astype(bf16), b.astype(bf16)], axis=1))
        rows_of = [[c, zero], [zero, d]] if w == 0 else [[c, d], [-d, c]]
        rhs.append(jnp.concatenate([jnp.concatenate(r, axis=1) for r in rows_of], axis=0))
    out = jnp.einsum("fgh,fhn->fgn", jnp.stack(lhs), jnp.stack(rhs), preferred_element_type=f32)
    out = out.astype(bf16).reshape(half, members, rows, 2 * vectors)
    out = lax.psum_scatter(out, "tr", scatter_dimension=1, tiled=True)[:, 0].astype(f32)
    parts = [(out[w, :, :vectors], out[w, :, vectors:]) for w in range(half)]
    freq = [(parts[0][0], None)] + parts[1:] + [(parts[0][1], None)]
    total = jnp.stack(backward(freq)) * (1.0 / total_k)
    potential = lax.all_to_all(total.astype(bf16), "blk", split_axis=0, concat_axis=1, tiled=True)

    direct = jnp.dot(masked, potential.reshape(kpoints * own_waves, vectors), preferred_element_type=f32)

    projected = jnp.einsum("tg,tn->gn", exchange_dens, trial, preferred_element_type=f32)
    projected = lax.psum_scatter(projected, "blk", scatter_dimension=0, tiled=True)
    part = projected.shape[0]
    own_coulomb = lax.dynamic_slice_in_dim(coulomb, group * part, part, 0)
    scaled = lax.all_gather((own_coulomb[:, None] * projected).astype(bf16), "blk", axis=0, tiled=True)
    exchange_term = jnp.dot(exchange_dens, scaled, preferred_element_type=f32)

    summed = lax.psum_scatter(2.0 * exchange_term - direct, "tr", scatter_dimension=0, tiled=True)
    row_count = summed.shape[0]
    own_trial = lax.dynamic_slice_in_dim(trial, member * row_count, row_count, 0)
    return energies[:, None] * own_trial.astype(f32) + summed


def solution(mesh):
    in_specs = (
        P("blk", None),
        P(("blk", "tr")),
        P("blk"),
        P("blk", "tr"),
        P("blk", "tr"),
        P("tr"),
        P("blk", None, "tr"),
    )
    out_specs = P(("blk", "tr"), None)
    return jax.shard_map(
        per_device, mesh=mesh, in_specs=in_specs, out_specs=out_specs, check_vma=False
    )
```

```python
import functools
import math

import jax
import jax.numpy as jnp
from jax import lax
from jax.experimental import pallas as pl
from jax.experimental.pallas import tpu as pltpu
from jax.sharding import PartitionSpec as P

F32, BF16 = jnp.float32, jnp.bfloat16
NT_DIMS = (((1,), (1,)), ((), ()))


def turn(value, angle):
    re, im = value
    c, s = math.cos(angle), math.sin(angle)
    if abs(s) < 1e-9:
        return value
    if abs(c) < 1e-9:
        return (None if im is None else -s * im), s * re
    if im is None:
        return c * re, s * re
    return c * re - s * im, s * re + c * im


def plus(a, b):
    return b if a is None else a if b is None else a + b


def minus(a, b):
    return a if b is None else -b if a is None else a - b


def forward(x):
    n = len(x)
    if n == 2:
        return [(x[0] + x[1], None), (x[0] - x[1], None)]
    even, odd = forward(x[0::2]), forward(x[1::2])
    out = [None] * (n // 2 + 1)
    for w in range(n // 4 + 1):
        e, o = even[w], turn(odd[w], -2 * math.pi * w / n)
        out[w] = plus(e[0], o[0]), plus(e[1], o[1])
        if w != n // 2 - w:
            re, im = minus(e[0], o[0]), minus(e[1], o[1])
            out[n // 2 - w] = re, None if im is None else -im
    return out


def backward(y):
    n = 2 * (len(y) - 1)
    if n == 2:
        return [y[0][0] + y[1][0], y[0][0] - y[1][0]]
    even, odd = [], []
    for w in range(n // 4 + 1):
        a, b = y[w], y[n // 2 - w]
        even.append((plus(a[0], b[0]), minus(a[1], b[1])))
        odd.append(turn((minus(a[0], b[0]), plus(a[1], b[1])), 2 * math.pi * w / n))
    for part in (even, odd):
        part[0], part[-1] = (part[0][0], None), (part[-1][0], None)
    out = [None] * n
    out[0::2], out[1::2] = backward(even), backward(odd)
    return out


def wait_bytes(ref, sem):
    pltpu.make_async_copy(ref, ref, sem).wait()


def send(src, dst, send_sem, recv_sem, device):
    pltpu.make_async_remote_copy(
        src_ref=src, dst_ref=dst, send_sem=send_sem, recv_sem=recv_sem,
        device_id=device, device_id_type=pl.DeviceIdType.MESH,
    ).start()


def kernel(
    sizes, s_hbm, e_hbm, d_hbm, t_hbm, kp, coul, out,
    e, d, t, tt, d2, s_in, b_out, b_in, rhs, lhs, part, core_in, ring_out, ring_in,
    proj, proj_in, scaled, eterm, p_out, p_in, prhs, f_part, f_core, t_out, t_in,
    sem_load, sem_s_out, sem_s_in, sem_b, sem_x, sem_c_out, sem_c_in, sem_r_out, sem_r_in,
    sem_p, sem_f_out, sem_f_in, sem_t,
):
    groups, zs, kpts, rows, waves, vecs, parts = sizes
    total_k = groups * kpts
    half = total_k // 2
    step = half // parts
    gb = lax.axis_index("blk")
    me = lax.axis_index("tr")
    z, xh, c = me // 4, (me // 2) % 2, me % 2

    def place(zz, xx, cc):
        return zz * 4 + xx * 2 + cc

    other = {"tr": place(z, xh, 1 - c)}
    onward = {"tr": place((z + 1 - 2 * c + zs) % zs, xh, c)}

    loads = [pltpu.make_async_copy(a, b, sem_load.at[i]) for i, (a, b) in enumerate(((t_hbm, t), (d_hbm, d), (e_hbm, e)))]
    for load in loads:
        load.start()

    barrier = pltpu.get_barrier_semaphore()

    def greet(device):
        pl.semaphore_signal(barrier, inc=1, device_id=device, device_id_type=pl.DeviceIdType.MESH)

    greet(other)

    def greet_blk(i, carry):
        greet({"blk": (gb + i // 2) % groups, "tr": place(z, (xh + i) % 2, c)})
        return carry

    def greet_tr(i, carry):
        greet({"tr": place((z + i // 2) % zs, (xh + i) % 2, c)})
        return carry

    lax.fori_loop(1, 2 * groups, greet_blk, 0)
    lax.fori_loop(1, 2 * zs, greet_tr, 0)

    ring_in[0] = jnp.zeros(ring_in.shape[1:], BF16)
    loads[0].wait()
    count = t.shape[0]
    unit = min(128, count)
    tt[...] = t[...].T
    loads[1].wait()
    eye = lax.broadcasted_iota(jnp.int32, (unit, unit), 0) == lax.broadcasted_iota(jnp.int32, (unit, unit), 1)
    for i in range(count // unit):
        local = (kp[:, i * unit : (i + 1) * unit] - gb * kpts).astype(F32)
        column = jnp.sum(jnp.where(eye, jnp.broadcast_to(local, (unit, unit)), 0.0), axis=1, keepdims=True)
        dens = d[i * unit : (i + 1) * unit, :].astype(F32)
        for k in range(kpts):
            mask = jnp.where(column == float(k), 1.0, 0.0)
            d2[i * unit : (i + 1) * unit, k * waves : (k + 1) * waves] = (dens * mask).astype(BF16)
    own = jnp.dot(tt[...], d2[...], preferred_element_type=F32)
    for k in range(kpts):
        b_out[k] = own[:, k * waves : (k + 1) * waves].astype(BF16)

    pl.semaphore_wait(barrier, 2 * groups + 2 * zs - 1)

    def send_s(stage, carry):
        for ab, zz in enumerate(((z - 1 - stage + 2 * zs) % zs, (z + 1 + stage) % zs)):
            pltpu.make_async_copy(s_hbm.at[:, zz, :, ab, gb], s_in.at[stage, gb, ab], sem_s_in.at[stage]).start()

        def to_peer(i, inner):
            peer = (gb + i) % groups
            for ab, zz in enumerate(((z - 1 - stage + 2 * zs) % zs, (z + 1 + stage) % zs)):
                send(s_hbm.at[:, zz, :, ab, peer], s_in.at[stage, gb, ab], sem_s_out.at[stage], sem_s_in.at[stage], {"blk": peer})
            return inner

        return lax.fori_loop(1, groups, to_peer, carry)

    send_s(0, 0)
    pltpu.make_async_copy(b_out, b_in.at[gb], sem_b.at[1]).start()

    def send_b(i, carry):
        send(b_out, b_in.at[gb], sem_b.at[0], sem_b.at[1], {"blk": (gb + i) % groups})
        return carry

    lax.fori_loop(1, groups, send_b, 0)
    send_s(1, 0)

    loads[2].wait()
    own_waves = e.shape[1]
    share = own_waves // groups
    chunk = min(256, own_waves)
    for i in range(own_waves // chunk):
        cols = slice(i * chunk, (i + 1) * chunk)
        proj[:, cols] = jnp.dot(tt[...], e[:, cols], preferred_element_type=F32).astype(BF16)

    def cut(index):
        return pl.ds(pl.multiple_of(index * share, share), share)

    pltpu.make_async_copy(proj.at[:, cut(gb)], proj_in.at[gb], sem_x.at[1]).start()

    def send_proj(i, carry):
        peer = (gb + i) % groups
        send(proj.at[:, cut(peer)], proj_in.at[gb], sem_x.at[0], sem_x.at[1], {"blk": peer})
        return carry

    lax.fori_loop(1, groups, send_proj, 0)
    lax.fori_loop(2, zs, send_s, 0)

    wait_bytes(b_in, sem_b.at[1])
    tile = min(16, vecs)

    def transform_b(i, carry):
        at = pl.ds(pl.multiple_of(i * tile, tile), tile)
        low = pl.ds(pl.multiple_of(vecs + i * tile, tile), tile)
        freq = forward([b_in[q // kpts, q % kpts, at, :].astype(F32) for q in range(total_k)])
        zero = jnp.zeros((tile, waves), BF16)
        for f in range(half):
            re, im = (freq[0][0], freq[half][0]) if f == 0 else freq[f]
            re, im = re.astype(BF16), im.astype(BF16)
            rhs[f, at, 0:waves] = re
            rhs[f, at, waves:] = zero if f == 0 else -im
            rhs[f, low, 0:waves] = zero if f == 0 else im
            rhs[f, low, waves:] = im if f == 0 else re
        return carry

    lax.fori_loop(0, vecs // tile, transform_b, 0)

    def multiply(stage):
        wait_bytes(s_in.at[stage], sem_s_in.at[stage])
        for ab in range(2):
            for xx in range(2):
                freq = forward([s_in[stage, q // kpts, ab, q % kpts, xx].astype(F32) for q in range(total_k)])
                at = slice((ab * 2 + xx) * rows, (ab * 2 + xx + 1) * rows)
                for f in range(half):
                    re, im = (freq[0][0], freq[half][0]) if f == 0 else freq[f]
                    lhs[f, at, 0:waves] = re.astype(BF16)
                    lhs[f, at, waves:] = im.astype(BF16)
        for p in range(parts):
            for f in range(p * step, (p + 1) * step):
                value = lax.dot_general(lhs[f], rhs[f], NT_DIMS, preferred_element_type=F32)
                part[stage, 0, f] = value[: 2 * rows].astype(BF16)
                part[stage, 1, f] = value[2 * rows :].astype(BF16)
            cut_f = pl.ds(p * step, step)
            send(part.at[stage, 1 - c, cut_f], core_in.at[stage, cut_f], sem_c_out.at[stage], sem_c_in.at[stage, p], other)

    def pass_on(stage):
        for p in range(parts):
            cut_f = pl.ds(p * step, step)
            wait_bytes(core_in.at[stage, cut_f], sem_c_in.at[stage, p])

            @pl.when(stage > 0)
            def _():
                wait_bytes(ring_in.at[stage, cut_f], sem_r_in.at[stage, p])

            for f in range(p * step, (p + 1) * step):
                value = part[stage, c, f].astype(F32) + core_in[stage, f].astype(F32) + ring_in[stage, f].astype(F32)
                ring_out[stage, f] = value.astype(BF16)

            @pl.when(stage < zs - 1)
            def _():
                send(ring_out.at[stage, cut_f], ring_in.at[stage + 1, cut_f], sem_r_out.at[stage], sem_r_in.at[stage + 1, p], onward)

    def reduce_projection():
        wait_bytes(proj_in, sem_x.at[1])
        total = proj_in[0].astype(F32)
        for i in range(1, groups):
            total = total + proj_in[i].astype(F32)
        scaled[:, cut(gb)] = (coul[pl.ds(gb, 1), :] * total).astype(BF16)

        def send_scaled(i, carry):
            send(scaled.at[:, cut(gb)], scaled.at[:, cut(gb)], sem_x.at[2], sem_x.at[3], {"blk": (gb + i) % groups})
            return carry

        lax.fori_loop(1, groups, send_scaled, 0)

    def exchange():
        wait_bytes(scaled.at[:, pl.ds(0, (groups - 1) * share)], sem_x.at[3])
        chunk_t = min(256, count)

        def do(i, carry):
            at = pl.ds(pl.multiple_of(i * chunk_t, chunk_t), chunk_t)
            eterm[at, :] = 2.0 * lax.dot_general(e[at, :], scaled[...], NT_DIMS, preferred_element_type=F32)
            return carry

        lax.fori_loop(0, count // chunk_t, do, 0)

    def stage_step(stage, carry):
        @pl.when(stage < zs)
        def _():
            multiply(stage)

        @pl.when(stage > 0)
        def _():
            pass_on(stage - 1)

        @pl.when(stage == min(3, zs - 1))
        def _():
            reduce_projection()

        @pl.when(stage == zs - 1)
        def _():
            exchange()

        return carry

    lax.fori_loop(0, zs + 1, stage_step, 0)

    lane = min(128, vecs)
    for xx in range(2):
        at = slice(xx * rows, (xx + 1) * rows)
        for n in range(vecs // lane):
            re = slice(n * lane, (n + 1) * lane)
            im = slice(vecs + n * lane, vecs + (n + 1) * lane)
            both = [(ring_out[zs - 1, f, at, re].astype(F32), ring_out[zs - 1, f, at, im].astype(F32)) for f in range(half)]
            values = backward([(both[0][0], None)] + both[1:] + [(both[0][1], None)])
            for k in range(total_k):
                p_out[xx, k // kpts, k % kpts, :, re] = (values[k] * (1.0 / total_k)).astype(BF16)
    pltpu.make_async_copy(p_out.at[xh, gb], p_in.at[gb, xh], sem_p.at[1]).start()

    def send_p(i, carry):
        peer, xx = (gb + i // 2) % groups, (xh + i) % 2
        send(p_out.at[xx, peer], p_in.at[gb, xh], sem_p.at[0], sem_p.at[1], {"blk": peer, "tr": place(z, xx, c)})
        return carry

    lax.fori_loop(1, 2 * groups, send_p, 0)
    wait_bytes(p_in, sem_p.at[1])
    for k in range(kpts):
        for g in range(groups):
            value = p_in[g, 0, k].astype(F32) + p_in[g, 1, k].astype(F32)
            prhs[(k * groups + g) * rows : (k * groups + g + 1) * rows, :] = value.astype(BF16)

    own_t = count // (4 * zs)
    for m in range(zs // 2):
        at = slice(m * 8 * own_t, (m + 1) * 8 * own_t)
        value = eterm[at, :] - jnp.dot(d2[at, :], prhs[...], preferred_element_type=F32)
        for i in range(8):
            f_part[i % 2, m * 2 + i // 4, i // 2 % 2] = value[i * own_t : (i + 1) * own_t]
        pair = pl.ds(m * 2, 2)
        send(f_part.at[1 - c, pair], f_core.at[pair], sem_f_out, sem_f_in.at[m], other)
    for m in range(zs // 2):
        pair = pl.ds(m * 2, 2)
        wait_bytes(f_core.at[pair], sem_f_in.at[m])
        t_out[pair] = (f_part[c, pair] + f_core[pair]).astype(BF16)
    pltpu.make_async_copy(t_out.at[z, xh], t_in.at[z, xh], sem_t.at[1]).start()

    def send_t(i, carry):
        zz, xx = (z + i // 2) % zs, (xh + i) % 2
        send(t_out.at[zz, xx], t_in.at[z, xh], sem_t.at[0], sem_t.at[1], {"tr": place(zz, xx, c)})
        return carry

    lax.fori_loop(1, 2 * zs, send_t, 0)
    wait_bytes(t_in, sem_t.at[1])
    total = jnp.zeros(out.shape, F32)
    for zz in range(zs):
        for xx in range(2):
            total = total + t_in[zz, xx].astype(F32)
    out[...] = total

    def sent_stage(stage, carry):
        wait_bytes(s_in.at[stage, pl.ds(0, groups - 1)], sem_s_out.at[stage])
        wait_bytes(core_in.at[stage], sem_c_out.at[stage])

        @pl.when(stage < zs - 1)
        def _():
            wait_bytes(ring_out.at[stage], sem_r_out.at[stage])

        return carry

    lax.fori_loop(0, zs, sent_stage, 0)
    wait_bytes(b_in.at[pl.ds(0, groups - 1)], sem_b.at[0])
    wait_bytes(proj_in.at[pl.ds(0, groups - 1)], sem_x.at[0])
    wait_bytes(proj_in.at[pl.ds(0, groups - 1)], sem_x.at[2])
    wait_bytes(p_in.at[pl.ds(0, groups - 1)], sem_p.at[0])
    wait_bytes(p_in.at[0, 0], sem_p.at[0])
    wait_bytes(f_core, sem_f_out)
    wait_bytes(t_in.at[pl.ds(0, zs - 1)], sem_t.at[0])
    wait_bytes(t_in.at[0, 0], sem_t.at[0])


def per_device(trial, energies, kpoint_of, exchange_dens, direct_dens, coulomb, screened):
    groups, members = lax.axis_size("blk"), lax.axis_size("tr")
    member = lax.axis_index("tr")
    kpts, all_waves, waves = screened.shape
    count, vecs = trial.shape
    zs = members // 4
    rows = all_waves // groups // members
    half = groups * kpts // 2
    own_waves = exchange_dens.shape[1]
    share = own_waves // groups
    own_t = count // members
    parts = min(4, half)
    dma, vmem = pltpu.SemaphoreType.DMA, pltpu.VMEM
    scratch = [
        vmem((count, own_waves), BF16),
        vmem((count, waves), BF16),
        vmem((count, vecs), BF16),
        vmem((vecs, count), BF16),
        vmem((count, kpts * waves), BF16),
        vmem((zs, groups, 2, kpts, 2, rows, waves), BF16),
        vmem((kpts, vecs, waves), BF16),
        vmem((groups, kpts, vecs, waves), BF16),
        vmem((half, 2 * vecs, 2 * waves), BF16),
        vmem((half, 4 * rows, 2 * waves), BF16),
        vmem((zs, 2, half, 2 * rows, 2 * vecs), BF16),
        vmem((zs, half, 2 * rows, 2 * vecs), BF16),
        vmem((zs, half, 2 * rows, 2 * vecs), BF16),
        vmem((zs, half, 2 * rows, 2 * vecs), BF16),
        vmem((vecs, own_waves), BF16),
        vmem((groups, vecs, share), BF16),
        vmem((vecs, own_waves), BF16),
        vmem((count, vecs), F32),
        vmem((2, groups, kpts, rows, vecs), BF16),
        vmem((groups, 2, kpts, rows, vecs), BF16),
        vmem((kpts * groups * rows, vecs), BF16),
        vmem((2, zs, 2, own_t, vecs), F32),
        vmem((zs, 2, own_t, vecs), F32),
        vmem((zs, 2, own_t, vecs), BF16),
        vmem((zs, 2, own_t, vecs), BF16),
        dma((3,)),
        dma((zs,)),
        dma((zs,)),
        dma((2,)),
        dma((4,)),
        dma((zs,)),
        dma((zs, parts)),
        dma((zs,)),
        dma((zs, parts)),
        dma((2,)),
        dma,
        dma((zs // 2,)),
        dma((2,)),
    ]
    anywhere, in_vmem = pl.BlockSpec(memory_space=pl.ANY), pl.BlockSpec(memory_space=pltpu.VMEM)
    summed = pl.pallas_call(
        functools.partial(kernel, (groups, zs, kpts, rows, waves, vecs, parts)),
        out_shape=jax.ShapeDtypeStruct((own_t, vecs), F32),
        in_specs=[anywhere] * 4 + [in_vmem] * 2,
        out_specs=in_vmem,
        scratch_shapes=scratch,
        compiler_params=pltpu.CompilerParams(collective_id=0, has_side_effects=True, vmem_limit_bytes=48 * 1024 * 1024),
    )(
        screened.reshape(kpts, zs, 2, 2, groups, rows, waves),
        exchange_dens,
        direct_dens,
        trial,
        kpoint_of.reshape(1, count),
        coulomb.reshape(groups, share),
    )
    own_trial = lax.dynamic_slice_in_dim(trial, member * own_t, own_t, 0)
    return energies[:, None] * own_trial.astype(F32) + summed


def solution(mesh):
    in_specs = (
        P("blk", None),
        P(("blk", "tr")),
        P("blk"),
        P("blk", "tr"),
        P("blk", "tr"),
        P("tr"),
        P("blk", None, "tr"),
    )
    out_specs = P(("blk", "tr"), None)
    return jax.shard_map(
        per_device, mesh=mesh, in_specs=in_specs, out_specs=out_specs, check_vma=False
    )
```

```python
import functools
import math

import jax
import jax.numpy as jnp
from jax import lax
from jax.experimental import pallas as pl
from jax.experimental.pallas import tpu as pltpu
from jax.sharding import PartitionSpec as P

F32, BF16 = jnp.float32, jnp.bfloat16
WINDOW, X_AFTER = 3, 4
NT_DIMS = (((1,), (1,)), ((), ()))


def turn(value, angle):
    re, im = value
    c, s = math.cos(angle), math.sin(angle)
    if abs(s) < 1e-9:
        return value
    if abs(c) < 1e-9:
        return (None if im is None else -s * im), s * re
    if im is None:
        return c * re, s * re
    return c * re - s * im, s * re + c * im


def plus(a, b):
    return b if a is None else a if b is None else a + b


def minus(a, b):
    return a if b is None else -b if a is None else a - b


def forward(x):
    n = len(x)
    if n == 2:
        return [(x[0] + x[1], None), (x[0] - x[1], None)]
    even, odd = forward(x[0::2]), forward(x[1::2])
    out = [None] * (n // 2 + 1)
    for w in range(n // 4 + 1):
        e, o = even[w], turn(odd[w], -2 * math.pi * w / n)
        out[w] = plus(e[0], o[0]), plus(e[1], o[1])
        if w != n // 2 - w:
            re, im = minus(e[0], o[0]), minus(e[1], o[1])
            out[n // 2 - w] = re, None if im is None else -im
    return out


def backward(y):
    n = 2 * (len(y) - 1)
    if n == 2:
        return [y[0][0] + y[1][0], y[0][0] - y[1][0]]
    even, odd = [], []
    for w in range(n // 4 + 1):
        a, b = y[w], y[n // 2 - w]
        even.append((plus(a[0], b[0]), minus(a[1], b[1])))
        odd.append(turn((minus(a[0], b[0]), plus(a[1], b[1])), 2 * math.pi * w / n))
    for part in (even, odd):
        part[0], part[-1] = (part[0][0], None), (part[-1][0], None)
    out = [None] * n
    out[0::2], out[1::2] = backward(even), backward(odd)
    return out


def wait_bytes(ref, sem):
    pltpu.make_async_copy(ref, ref, sem).wait()


def send(src, dst, send_sem, recv_sem, device):
    pltpu.make_async_remote_copy(
        src_ref=src, dst_ref=dst, send_sem=send_sem, recv_sem=recv_sem,
        device_id=device, device_id_type=pl.DeviceIdType.MESH,
    ).start()


def when(condition, do):
    if isinstance(condition, bool):
        if condition:
            do()
    else:

        @pl.when(condition)
        def _():
            do()


def kernel(
    sizes, s_hbm, e_hbm, d_hbm, t_hbm, kp, coul, out,
    e, d, t, tt, d2, s_in, b_out, b_in, rhs, lhs, part, core_in, ring_out, ring_in,
    proj, proj_out, pair_in, pair_out, proj_in, scaled, eterm, p_out, p_in, prhs, f_part, f_core, t_out, t_in,
    sem_load, sem_s_out, sem_s_in, sem_b_out, sem_b_in, sem_x, sem_c_out, sem_c_in, sem_r_out, sem_r_in,
    sem_p, sem_f, sem_t,
):
    groups, zs, kpts, rows, waves, vecs, parts, pieces = sizes
    lane = vecs // pieces
    ys = groups // 2
    total_k = groups * kpts
    half = total_k // 2
    units = pieces * half
    step = units // parts
    gb = lax.axis_index("blk")
    me = lax.axis_index("tr")
    z, xh, c = me // 4, (me // 2) % 2, me % 2
    y, xl = gb // 2, gb % 2
    beside = y * 2 + 1 - xl

    def place(zz, xx, cc):
        return zz * 4 + xx * 2 + cc

    def along(j):
        return (gb + 2 * j) % groups

    other = {"tr": place(z, xh, 1 - c)}
    onward = {"tr": place((z + 1 - 2 * c + zs) % zs, xh, c)}

    loads = [pltpu.make_async_copy(a, b, sem_load.at[i]) for i, (a, b) in enumerate(((t_hbm, t), (d_hbm, d), (e_hbm, e)))]
    for load in loads:
        load.start()

    barrier = pltpu.get_barrier_semaphore()

    def greet(device):
        pl.semaphore_signal(barrier, inc=1, device_id=device, device_id_type=pl.DeviceIdType.MESH)

    greet(other)

    def greet_blk(i, carry):
        greet({"blk": (gb + i // 2) % groups, "tr": place(z, (xh + i) % 2, c)})
        return carry

    def greet_tr(i, carry):
        greet({"tr": place((z + i // 2) % zs, (xh + i) % 2, c)})
        return carry

    lax.fori_loop(1, 2 * groups, greet_blk, 0)
    lax.fori_loop(1, 2 * zs, greet_tr, 0)
    loads[0].wait()
    count = t.shape[0]
    tt[...] = t[...].T
    pl.semaphore_wait(barrier, 2 * groups + 2 * zs - 1)

    def send_s(stage, carry):
        for ab, zz in enumerate(((z - 1 - stage + 2 * zs) % zs, (z + 1 + stage) % zs)):
            pltpu.make_async_copy(s_hbm.at[:, zz, :, ab, gb], s_in.at[stage, gb, ab], sem_s_in.at[stage]).start()

        def to_peer(i, inner):
            peer = (gb + i) % groups
            for ab, zz in enumerate(((z - 1 - stage + 2 * zs) % zs, (z + 1 + stage) % zs)):
                send(s_hbm.at[:, zz, :, ab, peer], s_in.at[stage, gb, ab], sem_s_out.at[stage], sem_s_in.at[stage], {"blk": peer})
            return inner

        return lax.fori_loop(1, groups, to_peer, carry)

    send_s(0, 0)

    loads[1].wait()
    local = (kp[...] - gb * kpts).astype(F32)
    for k in range(kpts):
        mask = jnp.where(local == float(k), 1.0, 0.0).astype(BF16)
        own = jnp.dot(tt[...] * mask, d[...], preferred_element_type=F32)
        for n in range(pieces):
            b_out[n, k] = own[n * lane : (n + 1) * lane].astype(BF16)
    rest = sem_b_in.at[ys]

    def send_block(src, slot, n, recv_sem, peer):
        send(src, b_in.at[slot, n], sem_b_out, recv_sem, {"blk": peer})

    send_block(b_out.at[0], gb, 0, sem_b_in.at[0], beside)
    for j in range(1, ys):
        send_block(b_out.at[1], gb, 1, sem_b_in.at[ys - j], along(j))
    send_block(b_out.at[1], gb, 1, rest, beside)
    for j in range(1, ys):
        send_block(b_out.at[0], gb, 0, rest, along(j))
    pltpu.make_async_copy(b_out, b_in.at[gb], rest).start()

    loads[2].wait()
    own_waves = e.shape[1]
    share = own_waves // groups
    for i in range(ys):
        value = jnp.dot(tt[...], e[:, 2 * i * share : 2 * (i + 1) * share], preferred_element_type=F32)
        for j in range(2):
            proj[i, j] = value[:, j * share : (j + 1) * share]
            proj_out[i, j] = value[:, j * share : (j + 1) * share].astype(BF16)

    wait_bytes(b_in.at[0, 0], sem_b_in.at[0])
    for j in range(1, ys):
        send_block(b_in.at[beside, 0], beside, 0, rest, along(j))
    for j in range(1, ys):
        wait_bytes(b_in.at[0, 1], sem_b_in.at[j])
        send_block(b_in.at[along(j), 1], along(j), 1, rest, beside)
    lax.fori_loop(1, min(WINDOW, zs), send_s, 0)

    ring_in[0] = jnp.zeros(ring_in.shape[1:], BF16)
    unit = min(128, count)
    eye = lax.broadcasted_iota(jnp.int32, (unit, unit), 0) == lax.broadcasted_iota(jnp.int32, (unit, unit), 1)
    for i in range(count // unit):
        at = slice(i * unit, (i + 1) * unit)
        column = jnp.sum(jnp.where(eye, jnp.broadcast_to(local[:, at], (unit, unit)), 0.0), axis=1, keepdims=True)
        dens = d[at, :].astype(F32)
        for k in range(kpts):
            d2[at, k * waves : (k + 1) * waves] = (dens * jnp.where(column == float(k), 1.0, 0.0)).astype(BF16)

    wait_bytes(b_in.at[pl.ds(0, 3 * ys // 2)], rest)
    tile = min(16, lane)

    def transform_b(i, carry):
        n, row = i // (lane // tile), i % (lane // tile) * tile
        at = pl.ds(pl.multiple_of(row, tile), tile)
        low = pl.ds(pl.multiple_of(lane + row, tile), tile)
        freq = forward([b_in[q // kpts, n, q % kpts, at, :].astype(F32) for q in range(total_k)])
        zero = jnp.zeros((tile, waves), BF16)
        for f in range(half):
            re, im = (freq[0][0], freq[half][0]) if f == 0 else freq[f]
            re, im = re.astype(BF16), im.astype(BF16)
            rhs[n, f, at, 0:waves] = re
            rhs[n, f, at, waves:] = zero if f == 0 else -im
            rhs[n, f, low, 0:waves] = zero if f == 0 else im
            rhs[n, f, low, waves:] = im if f == 0 else re
        return carry

    lax.fori_loop(0, vecs // tile, transform_b, 0)

    def cut(index):
        return pl.ds(pl.multiple_of(index * share, share), share)

    def send_pair():
        send(proj_out.at[:, 1 - xl], pair_in, sem_x.at[0], sem_x.at[1], {"blk": beside})

    def add_pair():
        wait_bytes(pair_in, sem_x.at[1])
        for i in range(ys):
            pair_out[i] = (proj[i, xl] + pair_in[i].astype(F32)).astype(BF16)
        for j in range(1, ys):
            send(pair_out.at[(y + j) % ys], proj_in.at[y], sem_x.at[2], sem_x.at[3], {"blk": along(j)})

    def add_projection():
        wait_bytes(proj_in.at[pl.ds(0, ys - 1)], sem_x.at[3])
        total = proj[y, xl] + pair_in[y].astype(F32)
        for j in range(1, ys):
            total = total + proj_in[(y + j) % ys].astype(F32)
        scaled[:, cut(gb)] = (coul[pl.ds(gb, 1), :] * total).astype(BF16)
        send(scaled.at[:, cut(gb)], scaled.at[:, cut(gb)], sem_x.at[4], sem_x.at[5], {"blk": beside})
        for j in range(1, ys):
            send(scaled.at[:, cut(gb)], scaled.at[:, cut(gb)], sem_x.at[4], sem_x.at[6], {"blk": along(j)})

    def forward_scaled():
        wait_bytes(scaled.at[:, pl.ds(0, share)], sem_x.at[5])
        for j in range(1, ys):
            send(scaled.at[:, cut(beside)], scaled.at[:, cut(beside)], sem_x.at[4], sem_x.at[6], {"blk": along(j)})

    def exchange():
        wait_bytes(scaled.at[:, pl.ds(0, (groups - 2) * share)], sem_x.at[6])
        chunk_t = min(256, count)

        def do(i, carry):
            at = pl.ds(pl.multiple_of(i * chunk_t, chunk_t), chunk_t)
            eterm[at, :] = 2.0 * lax.dot_general(e[at, :], scaled[...], NT_DIMS, preferred_element_type=F32)
            return carry

        lax.fori_loop(0, count // chunk_t, do, 0)

    def transform_s(stage):
        wait_bytes(s_in.at[stage], sem_s_in.at[stage])
        when(stage + WINDOW == max(WINDOW, min(X_AFTER, zs - 1)), send_pair)
        when(stage + WINDOW < zs, lambda: send_s(stage + WINDOW, 0))
        for ab in range(2):
            for xx in range(2):
                freq = forward([s_in[stage, q // kpts, ab, q % kpts, xx].astype(F32) for q in range(total_k)])
                at = slice((ab * 2 + xx) * rows, (ab * 2 + xx + 1) * rows)
                for f in range(half):
                    re, im = (freq[0][0], freq[half][0]) if f == 0 else freq[f]
                    lhs[f, at, 0:waves] = re.astype(BF16)
                    lhs[f, at, waves:] = im.astype(BF16)

    def multiply(stage, p):
        for u in range(p * step, (p + 1) * step):
            value = lax.dot_general(lhs[u % half], rhs[u // half, u % half], NT_DIMS, preferred_element_type=F32)
            part[stage, 0, u] = value[: 2 * rows].astype(BF16)
            part[stage, 1, u] = value[2 * rows :].astype(BF16)
        at = pl.ds(p * step, step)
        send(part.at[stage, 1 - c, at], core_in.at[stage, at], sem_c_out.at[stage], sem_c_in.at[stage, p], other)

    def pass_on(stage, p):
        at = pl.ds(p * step, step)
        wait_bytes(core_in.at[stage, at], sem_c_in.at[stage, p])
        when(stage > 0, lambda: wait_bytes(ring_in.at[stage, at], sem_r_in.at[stage, p]))
        for u in range(p * step, (p + 1) * step):
            value = part[stage, c, u].astype(F32) + core_in[stage, u].astype(F32) + ring_in[stage, u].astype(F32)
            ring_out[stage, u] = value.astype(BF16)
        if not isinstance(stage, int):
            send(ring_out.at[stage, at], ring_in.at[stage + 1, at], sem_r_out.at[stage], sem_r_in.at[stage + 1, p], onward)

    transform_s(0)
    for p in range(parts):
        multiply(0, p)

    def stage_step(stage, carry):
        when(stage == min(4, zs - 1), add_pair)
        when(stage == min(6, zs - 1), add_projection)
        when(stage == min(7, zs - 1), forward_scaled)
        transform_s(stage)
        for p in range(parts):
            multiply(stage, p)
            pass_on(stage - 1, p)
        return carry

    lax.fori_loop(1, zs, stage_step, 0)

    for n in range(pieces):
        for p in range(n * parts // pieces, (n + 1) * parts // pieces):
            pass_on(zs - 1, p)
        for xx in range(2):
            at = slice(xx * rows, (xx + 1) * rows)
            both = [
                (ring_out[zs - 1, n * half + f, at, :lane].astype(F32), ring_out[zs - 1, n * half + f, at, lane:].astype(F32))
                for f in range(half)
            ]
            values = backward([(both[0][0], None)] + both[1:] + [(both[0][1], None)])
            for k in range(total_k):
                p_out[n, xx, k // kpts, k % kpts] = (values[k] * (1.0 / total_k)).astype(BF16)
        pltpu.make_async_copy(p_out.at[n, xh, gb], p_in.at[n, gb, xh], sem_p.at[1, n]).start()

        def send_p(i, carry):
            peer, xx = (gb + i // 2) % groups, (xh + i) % 2
            send(p_out.at[n, xx, peer], p_in.at[n, gb, xh], sem_p.at[0, n], sem_p.at[1, n], {"blk": peer, "tr": place(z, xx, c)})
            return carry

        lax.fori_loop(1, 2 * groups, send_p, 0)

    exchange()

    own_t = count // (4 * zs)
    for n in range(pieces):
        cols = slice(n * lane, (n + 1) * lane)
        wait_bytes(p_in.at[n], sem_p.at[1, n])
        for k in range(kpts):
            for g in range(groups):
                value = p_in[n, g, 0, k].astype(F32) + p_in[n, g, 1, k].astype(F32)
                prhs[(k * groups + g) * rows : (k * groups + g + 1) * rows, cols] = value.astype(BF16)
        for m in range(zs // 2):
            at = slice(m * 8 * own_t, (m + 1) * 8 * own_t)
            value = eterm[at, cols] - jnp.dot(d2[at, :], prhs[:, cols], preferred_element_type=F32)
            for i in range(8):
                f_part[n, i % 2, m * 2 + i // 4, i // 2 % 2] = value[i * own_t : (i + 1) * own_t]
        send(f_part.at[n, 1 - c], f_core.at[n], sem_f.at[0, n], sem_f.at[1, n], other)
    for n in range(pieces):
        wait_bytes(f_core.at[n], sem_f.at[1, n])
        t_out[n] = (f_part[n, c] + f_core[n]).astype(BF16)
        pltpu.make_async_copy(t_out.at[n, z, xh], t_in.at[n, z, xh], sem_t.at[1, n]).start()

        def send_t(i, carry):
            zz, xx = (z + i // 2) % zs, (xh + i) % 2
            send(t_out.at[n, zz, xx], t_in.at[n, z, xh], sem_t.at[0, n], sem_t.at[1, n], {"tr": place(zz, xx, c)})
            return carry

        lax.fori_loop(1, 2 * zs, send_t, 0)
    for n in range(pieces):
        wait_bytes(t_in.at[n], sem_t.at[1, n])
        total = jnp.zeros((own_t, lane), F32)
        for zz in range(zs):
            for xx in range(2):
                total = total + t_in[n, zz, xx].astype(F32)
        out[:, n * lane : (n + 1) * lane] = total

    def sent_stage(stage, carry):
        wait_bytes(s_in.at[stage, pl.ds(0, groups - 1)], sem_s_out.at[stage])
        wait_bytes(core_in.at[stage], sem_c_out.at[stage])

        @pl.when(stage < zs - 1)
        def _():
            wait_bytes(ring_out.at[stage], sem_r_out.at[stage])

        return carry

    lax.fori_loop(0, zs, sent_stage, 0)
    wait_bytes(b_in.at[pl.ds(0, groups - 1)], sem_b_out)
    wait_bytes(pair_in, sem_x.at[0])
    wait_bytes(proj_in.at[pl.ds(0, ys - 1)], sem_x.at[2])
    wait_bytes(scaled.at[:, pl.ds(0, (groups - 1) * share)], sem_x.at[4])
    for n in range(pieces):
        wait_bytes(p_in.at[n, pl.ds(0, groups - 1)], sem_p.at[0, n])
        wait_bytes(p_in.at[n, 0, 0], sem_p.at[0, n])
        wait_bytes(f_core.at[n], sem_f.at[0, n])
        wait_bytes(t_in.at[n, pl.ds(0, zs - 1)], sem_t.at[0, n])
        wait_bytes(t_in.at[n, 0, 0], sem_t.at[0, n])


def per_device(trial, energies, kpoint_of, exchange_dens, direct_dens, coulomb, screened):
    groups, members = lax.axis_size("blk"), lax.axis_size("tr")
    member = lax.axis_index("tr")
    kpts, all_waves, waves = screened.shape
    count, vecs = trial.shape
    zs = members // 4
    rows = all_waves // groups // members
    half = groups * kpts // 2
    own_waves = exchange_dens.shape[1]
    share = own_waves // groups
    own_t = count // members
    parts, pieces = 8, 2
    lane = vecs // pieces
    units = pieces * half
    ys = groups // 2
    dma, vmem = pltpu.SemaphoreType.DMA, pltpu.VMEM
    scratch = [
        vmem((count, own_waves), BF16),
        vmem((count, waves), BF16),
        vmem((count, vecs), BF16),
        vmem((vecs, count), BF16),
        vmem((count, kpts * waves), BF16),
        vmem((zs, groups, 2, kpts, 2, rows, waves), BF16),
        vmem((pieces, kpts, lane, waves), BF16),
        vmem((groups, pieces, kpts, lane, waves), BF16),
        vmem((pieces, half, 2 * lane, 2 * waves), BF16),
        vmem((half, 4 * rows, 2 * waves), BF16),
        vmem((zs, 2, units, 2 * rows, 2 * lane), BF16),
        vmem((zs, units, 2 * rows, 2 * lane), BF16),
        vmem((zs, units, 2 * rows, 2 * lane), BF16),
        vmem((zs, units, 2 * rows, 2 * lane), BF16),
        vmem((ys, 2, vecs, share), F32),
        vmem((ys, 2, vecs, share), BF16),
        vmem((ys, vecs, share), BF16),
        vmem((ys, vecs, share), BF16),
        vmem((ys, vecs, share), BF16),
        vmem((vecs, own_waves), BF16),
        vmem((count, vecs), F32),
        vmem((pieces, 2, groups, kpts, rows, lane), BF16),
        vmem((pieces, groups, 2, kpts, rows, lane), BF16),
        vmem((kpts * groups * rows, vecs), BF16),
        vmem((pieces, 2, zs, 2, own_t, lane), F32),
        vmem((pieces, zs, 2, own_t, lane), F32),
        vmem((pieces, zs, 2, own_t, lane), BF16),
        vmem((pieces, zs, 2, own_t, lane), BF16),
        dma((3,)),
        dma((zs,)),
        dma((zs,)),
        dma,
        dma((ys + 1,)),
        dma((7,)),
        dma((zs,)),
        dma((zs, parts)),
        dma((zs,)),
        dma((zs, parts)),
        dma((2, pieces)),
        dma((2, pieces)),
        dma((2, pieces)),
    ]
    anywhere, in_vmem = pl.BlockSpec(memory_space=pl.ANY), pl.BlockSpec(memory_space=pltpu.VMEM)
    summed = pl.pallas_call(
        functools.partial(kernel, (groups, zs, kpts, rows, waves, vecs, parts, pieces)),
        out_shape=jax.ShapeDtypeStruct((own_t, vecs), F32),
        in_specs=[anywhere] * 4 + [in_vmem] * 2,
        out_specs=in_vmem,
        scratch_shapes=scratch,
        compiler_params=pltpu.CompilerParams(collective_id=0, has_side_effects=True, vmem_limit_bytes=63 * 1024 * 1024),
    )(
        screened.reshape(kpts, zs, 2, 2, groups, rows, waves),
        exchange_dens,
        direct_dens,
        trial,
        kpoint_of.reshape(1, count),
        coulomb.reshape(groups, share),
    )
    own_trial = lax.dynamic_slice_in_dim(trial, member * own_t, own_t, 0)
    return energies[:, None] * own_trial.astype(F32) + summed


def solution(mesh):
    in_specs = (
        P("blk", None),
        P(("blk", "tr")),
        P("blk"),
        P("blk", "tr"),
        P("blk", "tr"),
        P("tr"),
        P("blk", None, "tr"),
    )
    out_specs = P(("blk", "tr"), None)
    return jax.shard_map(
        per_device, mesh=mesh, in_specs=in_specs, out_specs=out_specs, check_vma=False
    )
```

```python
import functools
import math

import jax
import jax.numpy as jnp
from jax import lax
from jax.experimental import pallas as pl
from jax.experimental.pallas import tpu as pltpu
from jax.sharding import PartitionSpec as P

F32, BF16 = jnp.float32, jnp.bfloat16
NT_DIMS = (((1,), (1,)), ((), ()))


def turn(value, angle):
    re, im = value
    c, s = math.cos(angle), math.sin(angle)
    if abs(s) < 1e-9:
        return value
    if abs(c) < 1e-9:
        return (None if im is None else -s * im), s * re
    if im is None:
        return c * re, s * re
    return c * re - s * im, s * re + c * im


def plus(a, b):
    return b if a is None else a if b is None else a + b


def minus(a, b):
    return a if b is None else -b if a is None else a - b


def forward(x):
    n = len(x)
    if n == 2:
        return [(x[0] + x[1], None), (x[0] - x[1], None)]
    even, odd = forward(x[0::2]), forward(x[1::2])
    out = [None] * (n // 2 + 1)
    for w in range(n // 4 + 1):
        e, o = even[w], turn(odd[w], -2 * math.pi * w / n)
        out[w] = plus(e[0], o[0]), plus(e[1], o[1])
        if w != n // 2 - w:
            re, im = minus(e[0], o[0]), minus(e[1], o[1])
            out[n // 2 - w] = re, None if im is None else -im
    return out


def backward(y):
    n = 2 * (len(y) - 1)
    if n == 2:
        return [y[0][0] + y[1][0], y[0][0] - y[1][0]]
    even, odd = [], []
    for w in range(n // 4 + 1):
        a, b = y[w], y[n // 2 - w]
        even.append((plus(a[0], b[0]), minus(a[1], b[1])))
        odd.append(turn((minus(a[0], b[0]), plus(a[1], b[1])), 2 * math.pi * w / n))
    for part in (even, odd):
        part[0], part[-1] = (part[0][0], None), (part[-1][0], None)
    out = [None] * n
    out[0::2], out[1::2] = backward(even), backward(odd)
    return out


def wait_bytes(ref, sem):
    pltpu.make_async_copy(ref, ref, sem).wait()


def send(src, dst, send_sem, recv_sem, device):
    pltpu.make_async_remote_copy(
        src_ref=src, dst_ref=dst, send_sem=send_sem, recv_sem=recv_sem,
        device_id=device, device_id_type=pl.DeviceIdType.MESH,
    ).start()


def when(condition, do):
    if isinstance(condition, bool):
        if condition:
            do()
    else:

        @pl.when(condition)
        def _():
            do()


def kernel(
    sizes, s_hbm, e_hbm, d_hbm, t_hbm, kp, coul, en, out,
    e, d, t, tt, d2, s_in, b_out, b_in, rhs, lhs, part, core_in, ring_out, ring_in,
    proj, proj_out, proj_in, scaled, eterm, p_out, p_in, prhs, f_part, f_core, t_out, t_in,
    sem_load, sem_s_out, sem_s_in, sem_b_out, sem_b_in, sem_x, sem_c_out, sem_c_in, sem_r_out, sem_r_in,
    sem_p, sem_f, sem_t,
):
    groups, zs, kpts, rows, waves, vecs, parts, pieces = sizes
    lane = vecs // pieces
    ys = groups // 2
    total_k = groups * kpts
    half = total_k // 2
    units = pieces * half
    step = units // parts
    gb = lax.axis_index("blk")
    me = lax.axis_index("tr")
    z, xh, c = me // 4, (me // 2) % 2, me % 2
    y, xl = gb // 2, gb % 2
    beside = y * 2 + 1 - xl

    def place(zz, xx, cc):
        return zz * 4 + xx * 2 + cc

    def along(j):
        return (gb + 2 * j) % groups

    other = {"tr": place(z, xh, 1 - c)}
    onward = {"tr": place((z + 1 - 2 * c + zs) % zs, xh, c)}

    loads = [pltpu.make_async_copy(a, b, sem_load.at[i]) for i, (a, b) in enumerate(((t_hbm, t), (d_hbm, d), (e_hbm, e)))]
    for load in loads:
        load.start()

    barrier = pltpu.get_barrier_semaphore()

    def greet(device):
        pl.semaphore_signal(barrier, inc=1, device_id=device, device_id_type=pl.DeviceIdType.MESH)

    greet(other)

    def greet_blk(i, carry):
        greet({"blk": (gb + i // 2) % groups, "tr": place(z, (xh + i) % 2, c)})
        return carry

    def greet_tr(i, carry):
        greet({"tr": place((z + i // 2) % zs, (xh + i) % 2, c)})
        return carry

    lax.fori_loop(1, 2 * groups, greet_blk, 0)
    lax.fori_loop(1, 2 * zs, greet_tr, 0)
    loads[0].wait()
    count = t.shape[0]
    tt[...] = t[...].T
    loads[1].wait()
    local = (kp[...] - gb * kpts).astype(F32)
    for k in range(kpts):
        mask = jnp.where(local == float(k), 1.0, 0.0).astype(BF16)
        own = jnp.dot(tt[...] * mask, d[...], preferred_element_type=F32)
        for n in range(pieces):
            b_out[n, k] = own[n * lane : (n + 1) * lane].astype(BF16)

    pl.semaphore_wait(barrier, 2 * groups + 2 * zs - 1)

    def send_s(stage, carry):
        for ab, zz in enumerate(((z - 1 - stage + 2 * zs) % zs, (z + 1 + stage) % zs)):
            pltpu.make_async_copy(s_hbm.at[:, zz, :, ab, gb], s_in.at[stage, gb, ab], sem_s_in.at[stage]).start()

        def to_peer(i, inner):
            peer = (gb + i) % groups
            for ab, zz in enumerate(((z - 1 - stage + 2 * zs) % zs, (z + 1 + stage) % zs)):
                send(s_hbm.at[:, zz, :, ab, peer], s_in.at[stage, gb, ab], sem_s_out.at[stage], sem_s_in.at[stage], {"blk": peer})
            return inner

        return lax.fori_loop(1, groups, to_peer, carry)

    rest = sem_b_in.at[ys]

    def send_block(src, slot, n, recv_sem, peer):
        send(src, b_in.at[slot, n], sem_b_out, recv_sem, {"blk": peer})

    send_block(b_out.at[0], gb, 0, sem_b_in.at[0], beside)
    for j in range(1, ys):
        send_block(b_out.at[1], gb, 1, sem_b_in.at[ys - j], along(j))
    send_block(b_out.at[1], gb, 1, rest, beside)
    for j in range(1, ys):
        send_block(b_out.at[0], gb, 0, rest, along(j))
    pltpu.make_async_copy(b_out, b_in.at[gb], rest).start()
    send_s(0, 0)

    loads[2].wait()
    own_waves = e.shape[1]
    share = own_waves // groups
    for i in range(ys):
        value = jnp.dot(tt[...], e[:, 2 * i * share : 2 * (i + 1) * share], preferred_element_type=F32)
        for j in range(2):
            proj[i, j] = value[:, j * share : (j + 1) * share]
            proj_out[i, j] = value[:, j * share : (j + 1) * share].astype(BF16)

    wait_bytes(b_in.at[0, 0], sem_b_in.at[0])
    for j in range(1, ys):
        send_block(b_in.at[beside, 0], beside, 0, rest, along(j))
    for j in range(1, ys):
        wait_bytes(b_in.at[0, 1], sem_b_in.at[j])
        send_block(b_in.at[along(j), 1], along(j), 1, rest, beside)

    def cut(index):
        return pl.ds(pl.multiple_of(index * share, share), share)

    def send_projection():
        for i in range(1, groups):
            peer = (gb + i) % groups
            send(proj_out.at[peer // 2, peer % 2], proj_in.at[gb], sem_x.at[0], sem_x.at[1], {"blk": peer})

    def add_projection():
        wait_bytes(proj_in.at[pl.ds(0, groups - 1)], sem_x.at[1])
        total = proj[y, xl]
        for i in range(1, groups):
            total = total + proj_in[(gb + i) % groups].astype(F32)
        scaled[:, cut(gb)] = (coul[pl.ds(gb, 1), :] * total).astype(BF16)
        for i in range(1, groups):
            send(scaled.at[:, cut(gb)], scaled.at[:, cut(gb)], sem_x.at[2], sem_x.at[3], {"blk": (gb + i) % groups})

    lax.fori_loop(min(1, zs), min(8, zs), send_s, 0)
    send_projection()

    ring_in[0] = jnp.zeros(ring_in.shape[1:], BF16)
    unit = min(128, count)
    eye = lax.broadcasted_iota(jnp.int32, (unit, unit), 0) == lax.broadcasted_iota(jnp.int32, (unit, unit), 1)
    for i in range(count // unit):
        at = slice(i * unit, (i + 1) * unit)
        column = jnp.sum(jnp.where(eye, jnp.broadcast_to(local[:, at], (unit, unit)), 0.0), axis=1, keepdims=True)
        dens = d[at, :].astype(F32)
        for k in range(kpts):
            d2[at, k * waves : (k + 1) * waves] = (dens * jnp.where(column == float(k), 1.0, 0.0)).astype(BF16)

    wait_bytes(b_in.at[pl.ds(0, 3 * ys // 2)], rest)
    tile = min(16, lane)

    def transform_b(i, carry):
        n, row = i // (lane // tile), i % (lane // tile) * tile
        at = pl.ds(pl.multiple_of(row, tile), tile)
        low = pl.ds(pl.multiple_of(lane + row, tile), tile)
        freq = forward([b_in[q // kpts, n, q % kpts, at, :].astype(F32) for q in range(total_k)])
        zero = jnp.zeros((tile, waves), BF16)
        for f in range(half):
            re, im = (freq[0][0], freq[half][0]) if f == 0 else freq[f]
            re, im = re.astype(BF16), im.astype(BF16)
            rhs[n, f, at, 0:waves] = re
            rhs[n, f, at, waves:] = zero if f == 0 else -im
            rhs[n, f, low, 0:waves] = zero if f == 0 else im
            rhs[n, f, low, waves:] = im if f == 0 else re
        return carry

    lax.fori_loop(0, vecs // tile, transform_b, 0)

    def exchange():
        wait_bytes(scaled.at[:, pl.ds(0, (groups - 1) * share)], sem_x.at[3])
        chunk_t = min(256, count)

        def do(i, carry):
            at = pl.ds(pl.multiple_of(i * chunk_t, chunk_t), chunk_t)
            eterm[at, :] = 2.0 * lax.dot_general(e[at, :], scaled[...], NT_DIMS, preferred_element_type=F32)
            return carry

        lax.fori_loop(0, count // chunk_t, do, 0)

    def transform_s(stage):
        wait_bytes(s_in.at[stage], sem_s_in.at[stage])
        for ab in range(2):
            for xx in range(2):
                freq = forward([s_in[stage, q // kpts, ab, q % kpts, xx].astype(F32) for q in range(total_k)])
                at = slice((ab * 2 + xx) * rows, (ab * 2 + xx + 1) * rows)
                for f in range(half):
                    re, im = (freq[0][0], freq[half][0]) if f == 0 else freq[f]
                    lhs[f, at, 0:waves] = re.astype(BF16)
                    lhs[f, at, waves:] = im.astype(BF16)

    def multiply(stage, p):
        for u in range(p * step, (p + 1) * step):
            value = lax.dot_general(lhs[u % half], rhs[u // half, u % half], NT_DIMS, preferred_element_type=F32)
            part[stage, 0, u] = value[: 2 * rows].astype(BF16)
            part[stage, 1, u] = value[2 * rows :].astype(BF16)
        at = pl.ds(p * step, step)
        send(part.at[stage, 1 - c, at], core_in.at[stage, at], sem_c_out.at[stage], sem_c_in.at[stage, p], other)

    def pass_on(stage, p):
        at = pl.ds(p * step, step)
        wait_bytes(core_in.at[stage, at], sem_c_in.at[stage, p])
        when(stage > 0, lambda: wait_bytes(ring_in.at[stage, at], sem_r_in.at[stage, p]))
        for u in range(p * step, (p + 1) * step):
            value = part[stage, c, u].astype(F32) + core_in[stage, u].astype(F32) + ring_in[stage, u].astype(F32)
            ring_out[stage, u] = value.astype(BF16)
        if not isinstance(stage, int):
            send(ring_out.at[stage, at], ring_in.at[stage + 1, at], sem_r_out.at[stage], sem_r_in.at[stage + 1, p], onward)

    transform_s(0)
    for p in range(parts):
        multiply(0, p)

    def stage_step(stage, carry):
        when(stage == min(7, zs - 1), add_projection)
        transform_s(stage)
        for p in range(parts):
            multiply(stage, p)
            pass_on(stage - 1, p)
        return carry

    lax.fori_loop(1, zs, stage_step, 0)

    for n in range(pieces):
        for p in range(n * parts // pieces, (n + 1) * parts // pieces):
            pass_on(zs - 1, p)
        for xx in range(2):
            at = slice(xx * rows, (xx + 1) * rows)
            both = [
                (ring_out[zs - 1, n * half + f, at, :lane].astype(F32), ring_out[zs - 1, n * half + f, at, lane:].astype(F32))
                for f in range(half)
            ]
            values = backward([(both[0][0], None)] + both[1:] + [(both[0][1], None)])
            for k in range(total_k):
                p_out[n, xx, k // kpts, k % kpts] = (values[k] * (1.0 / total_k)).astype(BF16)
        pltpu.make_async_copy(p_out.at[n, xh, gb], p_in.at[n, gb, xh], sem_p.at[1, n]).start()

        def send_p(i, carry):
            peer, xx = (gb + i // 2) % groups, (xh + i) % 2
            send(p_out.at[n, xx, peer], p_in.at[n, gb, xh], sem_p.at[0, n], sem_p.at[1, n], {"blk": peer, "tr": place(z, xx, c)})
            return carry

        lax.fori_loop(1, 2 * groups, send_p, 0)

    exchange()

    own_t = count // (4 * zs)
    for n in range(pieces):
        cols = slice(n * lane, (n + 1) * lane)
        wait_bytes(p_in.at[n], sem_p.at[1, n])
        for k in range(kpts):
            for g in range(groups):
                value = p_in[n, g, 0, k].astype(F32) + p_in[n, g, 1, k].astype(F32)
                prhs[(k * groups + g) * rows : (k * groups + g + 1) * rows, cols] = value.astype(BF16)
        for m in range(zs // 2):
            at = slice(m * 8 * own_t, (m + 1) * 8 * own_t)
            value = eterm[at, cols] - jnp.dot(d2[at, :], prhs[:, cols], preferred_element_type=F32)
            for i in range(8):
                f_part[n, i % 2, m * 2 + i // 4, i // 2 % 2] = value[i * own_t : (i + 1) * own_t]
        send(f_part.at[n, 1 - c], f_core.at[n], sem_f.at[0, n], sem_f.at[1, n], other)
    for n in range(pieces):
        wait_bytes(f_core.at[n], sem_f.at[1, n])
        t_out[n] = (f_part[n, c] + f_core[n]).astype(BF16)
        pltpu.make_async_copy(t_out.at[n, z, xh], t_in.at[n, z, xh], sem_t.at[1, n]).start()

        def send_t(i, carry):
            zz, xx = (z + i // 2) % zs, (xh + i) % 2
            send(t_out.at[n, zz, xx], t_in.at[n, z, xh], sem_t.at[0, n], sem_t.at[1, n], {"tr": place(zz, xx, c)})
            return carry

        lax.fori_loop(1, 2 * zs, send_t, 0)
    square = lax.broadcasted_iota(jnp.int32, (own_t, own_t), 0) == lax.broadcasted_iota(jnp.int32, (own_t, own_t), 1)
    level = jnp.sum(jnp.where(square, jnp.broadcast_to(en[...], (own_t, own_t)), 0.0), axis=1, keepdims=True)
    mine = pl.ds(pl.multiple_of(me * own_t, own_t), own_t)
    for n in range(pieces):
        total = level * t[mine, n * lane : (n + 1) * lane].astype(F32)
        wait_bytes(t_in.at[n], sem_t.at[1, n])
        for zz in range(zs):
            for xx in range(2):
                total = total + t_in[n, zz, xx].astype(F32)
        out[:, n * lane : (n + 1) * lane] = total

    def sent_stage(stage, carry):
        wait_bytes(s_in.at[stage, pl.ds(0, groups - 1)], sem_s_out.at[stage])
        wait_bytes(core_in.at[stage], sem_c_out.at[stage])

        @pl.when(stage < zs - 1)
        def _():
            wait_bytes(ring_out.at[stage], sem_r_out.at[stage])

        return carry

    lax.fori_loop(0, zs, sent_stage, 0)
    wait_bytes(b_in.at[pl.ds(0, groups - 1)], sem_b_out)
    wait_bytes(proj_in.at[pl.ds(0, groups - 1)], sem_x.at[0])
    wait_bytes(scaled.at[:, pl.ds(0, (groups - 1) * share)], sem_x.at[2])
    for n in range(pieces):
        wait_bytes(p_in.at[n, pl.ds(0, groups - 1)], sem_p.at[0, n])
        wait_bytes(p_in.at[n, 0, 0], sem_p.at[0, n])
        wait_bytes(f_core.at[n], sem_f.at[0, n])
        wait_bytes(t_in.at[n, pl.ds(0, zs - 1)], sem_t.at[0, n])
        wait_bytes(t_in.at[n, 0, 0], sem_t.at[0, n])


def per_device(trial, energies, kpoint_of, exchange_dens, direct_dens, coulomb, screened):
    groups, members = lax.axis_size("blk"), lax.axis_size("tr")
    kpts, all_waves, waves = screened.shape
    count, vecs = trial.shape
    zs = members // 4
    rows = all_waves // groups // members
    half = groups * kpts // 2
    own_waves = exchange_dens.shape[1]
    share = own_waves // groups
    own_t = count // members
    parts, pieces = 8, 2
    lane = vecs // pieces
    units = pieces * half
    ys = groups // 2
    dma, vmem = pltpu.SemaphoreType.DMA, pltpu.VMEM
    scratch = [
        vmem((count, own_waves), BF16),
        vmem((count, waves), BF16),
        vmem((count, vecs), BF16),
        vmem((vecs, count), BF16),
        vmem((count, kpts * waves), BF16),
        vmem((zs, groups, 2, kpts, 2, rows, waves), BF16),
        vmem((pieces, kpts, lane, waves), BF16),
        vmem((groups, pieces, kpts, lane, waves), BF16),
        vmem((pieces, half, 2 * lane, 2 * waves), BF16),
        vmem((half, 4 * rows, 2 * waves), BF16),
        vmem((zs, 2, units, 2 * rows, 2 * lane), BF16),
        vmem((zs, units, 2 * rows, 2 * lane), BF16),
        vmem((zs, units, 2 * rows, 2 * lane), BF16),
        vmem((zs, units, 2 * rows, 2 * lane), BF16),
        vmem((ys, 2, vecs, share), F32),
        vmem((ys, 2, vecs, share), BF16),
        vmem((groups, vecs, share), BF16),
        vmem((vecs, own_waves), BF16),
        vmem((count, vecs), F32),
        vmem((pieces, 2, groups, kpts, rows, lane), BF16),
        vmem((pieces, groups, 2, kpts, rows, lane), BF16),
        vmem((kpts * groups * rows, vecs), BF16),
        vmem((pieces, 2, zs, 2, own_t, lane), F32),
        vmem((pieces, zs, 2, own_t, lane), F32),
        vmem((pieces, zs, 2, own_t, lane), BF16),
        vmem((pieces, zs, 2, own_t, lane), BF16),
        dma((3,)),
        dma((zs,)),
        dma((zs,)),
        dma,
        dma((ys + 1,)),
        dma((4,)),
        dma((zs,)),
        dma((zs, parts)),
        dma((zs,)),
        dma((zs, parts)),
        dma((2, pieces)),
        dma((2, pieces)),
        dma((2, pieces)),
    ]
    anywhere, in_vmem = pl.BlockSpec(memory_space=pl.ANY), pl.BlockSpec(memory_space=pltpu.VMEM)
    return pl.pallas_call(
        functools.partial(kernel, (groups, zs, kpts, rows, waves, vecs, parts, pieces)),
        out_shape=jax.ShapeDtypeStruct((own_t, vecs), F32),
        in_specs=[anywhere] * 4 + [in_vmem] * 3,
        out_specs=in_vmem,
        scratch_shapes=scratch,
        compiler_params=pltpu.CompilerParams(collective_id=0, has_side_effects=True, vmem_limit_bytes=63 * 1024 * 1024),
    )(
        screened.reshape(kpts, zs, 2, 2, groups, rows, waves),
        exchange_dens,
        direct_dens,
        trial,
        kpoint_of.reshape(1, count),
        coulomb.reshape(groups, share),
        energies.reshape(1, own_t),
    )


def solution(mesh):
    in_specs = (
        P("blk", None),
        P(("blk", "tr")),
        P("blk"),
        P("blk", "tr"),
        P("blk", "tr"),
        P("tr"),
        P("blk", None, "tr"),
    )
    out_specs = P(("blk", "tr"), None)
    return jax.shard_map(
        per_device, mesh=mesh, in_specs=in_specs, out_specs=out_specs, check_vma=False
    )
```

```python
import functools
import math

import jax
import jax.numpy as jnp
from jax import lax
from jax.experimental import pallas as pl
from jax.experimental.pallas import tpu as pltpu
from jax.sharding import PartitionSpec as P

F32, BF16 = jnp.float32, jnp.bfloat16
NT_DIMS = (((1,), (1,)), ((), ()))


def turn(value, angle):
    re, im = value
    c, s = math.cos(angle), math.sin(angle)
    if abs(s) < 1e-9:
        return value
    if abs(c) < 1e-9:
        return (None if im is None else -s * im), s * re
    if im is None:
        return c * re, s * re
    return c * re - s * im, s * re + c * im


def plus(a, b):
    return b if a is None else a if b is None else a + b


def minus(a, b):
    return a if b is None else -b if a is None else a - b


def forward(x):
    n = len(x)
    if n == 2:
        return [(x[0] + x[1], None), (x[0] - x[1], None)]
    even, odd = forward(x[0::2]), forward(x[1::2])
    out = [None] * (n // 2 + 1)
    for w in range(n // 4 + 1):
        e, o = even[w], turn(odd[w], -2 * math.pi * w / n)
        out[w] = plus(e[0], o[0]), plus(e[1], o[1])
        if w != n // 2 - w:
            re, im = minus(e[0], o[0]), minus(e[1], o[1])
            out[n // 2 - w] = re, None if im is None else -im
    return out


def backward(y):
    n = 2 * (len(y) - 1)
    if n == 2:
        return [y[0][0] + y[1][0], y[0][0] - y[1][0]]
    even, odd = [], []
    for w in range(n // 4 + 1):
        a, b = y[w], y[n // 2 - w]
        even.append((plus(a[0], b[0]), minus(a[1], b[1])))
        odd.append(turn((minus(a[0], b[0]), plus(a[1], b[1])), 2 * math.pi * w / n))
    for part in (even, odd):
        part[0], part[-1] = (part[0][0], None), (part[-1][0], None)
    out = [None] * n
    out[0::2], out[1::2] = backward(even), backward(odd)
    return out


def wait_bytes(ref, sem):
    pltpu.make_async_copy(ref, ref, sem).wait()


def send(src, dst, send_sem, recv_sem, device):
    pltpu.make_async_remote_copy(
        src_ref=src, dst_ref=dst, send_sem=send_sem, recv_sem=recv_sem,
        device_id=device, device_id_type=pl.DeviceIdType.MESH,
    ).start()


def when(condition, do):
    if isinstance(condition, bool):
        if condition:
            do()
    else:

        @pl.when(condition)
        def _():
            do()


def kernel(
    sizes, s_hbm, e_hbm, d_hbm, t_hbm, kp, coul, en, out,
    e, d, t, tt, d2, s_in, b_out, b_in, rhs, lhs, part, core_in, ring_out, ring_in,
    proj, proj_out, proj_in, scaled, eterm, p_out, p_in, prhs, f_part, f_core, t_out, t_in,
    sem_load, sem_s_out, sem_s_in, sem_b_out, sem_b_in, sem_x, sem_c_out, sem_c_in, sem_r_out, sem_r_in,
    sem_p, sem_f, sem_t,
):
    groups, zs, kpts, rows, waves, vecs, parts, pieces = sizes
    lane = vecs // pieces
    ys = groups // 2
    total_k = groups * kpts
    half = total_k // 2
    units = pieces * half
    step = units // parts
    gb = lax.axis_index("blk")
    me = lax.axis_index("tr")
    z, xh, c = me // 4, (me // 2) % 2, me % 2
    y, xl = gb // 2, gb % 2
    beside = y * 2 + 1 - xl

    def place(zz, xx, cc):
        return zz * 4 + xx * 2 + cc

    def along(j):
        return (gb + 2 * j) % groups

    other = {"tr": place(z, xh, 1 - c)}
    onward = {"tr": place((z + 1 - 2 * c + zs) % zs, xh, c)}

    loads = [pltpu.make_async_copy(a, b, sem_load.at[i]) for i, (a, b) in enumerate(((t_hbm, t), (d_hbm, d), (e_hbm, e)))]
    for load in loads:
        load.start()

    barrier = pltpu.get_barrier_semaphore()

    def greet(device):
        pl.semaphore_signal(barrier, inc=1, device_id=device, device_id_type=pl.DeviceIdType.MESH)

    greet(other)

    def greet_blk(i, carry):
        greet({"blk": (gb + i // 2) % groups, "tr": place(z, (xh + i) % 2, c)})
        return carry

    def greet_tr(i, carry):
        greet({"tr": place((z + i // 2) % zs, (xh + i) % 2, c)})
        return carry

    lax.fori_loop(1, 2 * groups, greet_blk, 0)
    lax.fori_loop(1, 2 * zs, greet_tr, 0)
    loads[0].wait()
    count = t.shape[0]
    tt[...] = t[...].T
    loads[1].wait()
    local = (kp[...] - gb * kpts).astype(F32)
    for k in range(kpts):
        mask = jnp.where(local == float(k), 1.0, 0.0).astype(BF16)
        own = jnp.dot(tt[...] * mask, d[...], preferred_element_type=F32)
        for n in range(pieces):
            b_out[n, k] = own[n * lane : (n + 1) * lane].astype(BF16)

    pl.semaphore_wait(barrier, 2 * groups + 2 * zs - 1)

    def send_s(stage, carry):
        for ab, zz in enumerate(((z - 1 - stage + 2 * zs) % zs, (z + 1 + stage) % zs)):
            pltpu.make_async_copy(s_hbm.at[:, zz, :, ab, gb], s_in.at[stage, gb, ab], sem_s_in.at[stage]).start()

        def to_peer(i, inner):
            peer = (gb + i) % groups
            for ab, zz in enumerate(((z - 1 - stage + 2 * zs) % zs, (z + 1 + stage) % zs)):
                send(s_hbm.at[:, zz, :, ab, peer], s_in.at[stage, gb, ab], sem_s_out.at[stage], sem_s_in.at[stage], {"blk": peer})
            return inner

        return lax.fori_loop(1, groups, to_peer, carry)

    rest = sem_b_in.at[ys]

    def send_block(src, slot, n, recv_sem, peer):
        send(src, b_in.at[slot, n], sem_b_out, recv_sem, {"blk": peer})

    send_block(b_out.at[0], gb, 0, sem_b_in.at[0], beside)
    for j in range(1, ys):
        send_block(b_out.at[1], gb, 1, sem_b_in.at[ys - j], along(j))
    send_block(b_out.at[1], gb, 1, rest, beside)
    for j in range(1, ys):
        send_block(b_out.at[0], gb, 0, rest, along(j))
    pltpu.make_async_copy(b_out, b_in.at[gb], rest).start()
    send_s(0, 0)

    loads[2].wait()
    own_waves = e.shape[1]
    share = own_waves // groups
    for i in range(ys):
        value = jnp.dot(tt[...], e[:, 2 * i * share : 2 * (i + 1) * share], preferred_element_type=F32)
        for j in range(2):
            proj[i, j] = value[:, j * share : (j + 1) * share]
            proj_out[i, j] = value[:, j * share : (j + 1) * share].astype(BF16)

    wait_bytes(b_in.at[0, 0], sem_b_in.at[0])
    for j in range(1, ys):
        send_block(b_in.at[beside, 0], beside, 0, rest, along(j))
    for j in range(1, ys):
        wait_bytes(b_in.at[0, 1], sem_b_in.at[j])
        send_block(b_in.at[along(j), 1], along(j), 1, rest, beside)

    def cut(index):
        return pl.ds(pl.multiple_of(index * share, share), share)

    def send_projection():
        for i in range(1, groups):
            peer = (gb + i) % groups
            send(proj_out.at[peer // 2, peer % 2], proj_in.at[gb], sem_x.at[0], sem_x.at[1], {"blk": peer})

    def add_projection():
        wait_bytes(proj_in.at[pl.ds(0, groups - 1)], sem_x.at[1])
        total = proj[y, xl]
        for i in range(1, groups):
            total = total + proj_in[(gb + i) % groups].astype(F32)
        scaled[:, cut(gb)] = (coul[pl.ds(gb, 1), :] * total).astype(BF16)
        for i in range(1, groups):
            send(scaled.at[:, cut(gb)], scaled.at[:, cut(gb)], sem_x.at[2], sem_x.at[3], {"blk": (gb + i) % groups})

    lax.fori_loop(min(1, zs), min(8, zs), send_s, 0)
    send_projection()

    ring_in[0] = jnp.zeros(ring_in.shape[1:], BF16)
    unit = min(128, count)
    eye = lax.broadcasted_iota(jnp.int32, (unit, unit), 0) == lax.broadcasted_iota(jnp.int32, (unit, unit), 1)
    for i in range(count // unit):
        at = slice(i * unit, (i + 1) * unit)
        column = jnp.sum(jnp.where(eye, jnp.broadcast_to(local[:, at], (unit, unit)), 0.0), axis=1, keepdims=True)
        dens = d[at, :].astype(F32)
        for k in range(kpts):
            d2[at, k * waves : (k + 1) * waves] = (dens * jnp.where(column == float(k), 1.0, 0.0)).astype(BF16)

    wait_bytes(b_in.at[pl.ds(0, 3 * ys // 2)], rest)
    tile = min(16, lane)

    def transform_b(i, carry):
        n, row = i // (lane // tile), i % (lane // tile) * tile
        at = pl.ds(pl.multiple_of(row, tile), tile)
        low = pl.ds(pl.multiple_of(lane + row, tile), tile)
        freq = forward([b_in[q // kpts, n, q % kpts, at, :].astype(F32) for q in range(total_k)])
        zero = jnp.zeros((tile, waves), BF16)
        for f in range(half):
            re, im = (freq[0][0], freq[half][0]) if f == 0 else freq[f]
            re, im = re.astype(BF16), im.astype(BF16)
            rhs[n, f, at, 0:waves] = re
            rhs[n, f, at, waves:] = zero if f == 0 else -im
            rhs[n, f, low, 0:waves] = zero if f == 0 else im
            rhs[n, f, low, waves:] = im if f == 0 else re
        return carry

    lax.fori_loop(0, vecs // tile, transform_b, 0)

    def exchange():
        wait_bytes(scaled.at[:, pl.ds(0, (groups - 1) * share)], sem_x.at[3])
        chunk_t = min(256, count)

        def do(i, carry):
            at = pl.ds(pl.multiple_of(i * chunk_t, chunk_t), chunk_t)
            eterm[at, :] = 2.0 * lax.dot_general(e[at, :], scaled[...], NT_DIMS, preferred_element_type=F32)
            return carry

        lax.fori_loop(0, count // chunk_t, do, 0)

    def transform_s(stage):
        wait_bytes(s_in.at[stage], sem_s_in.at[stage])
        for ab in range(2):
            for xx in range(2):
                freq = forward([s_in[stage, q // kpts, ab, q % kpts, xx].astype(F32) for q in range(total_k)])
                at = slice((ab * 2 + xx) * rows, (ab * 2 + xx + 1) * rows)
                for f in range(half):
                    re, im = (freq[0][0], freq[half][0]) if f == 0 else freq[f]
                    lhs[f, at, 0:waves] = re.astype(BF16)
                    lhs[f, at, waves:] = im.astype(BF16)

    def multiply(stage, p):
        for u in range(p * step, (p + 1) * step):
            value = lax.dot_general(lhs[u % half], rhs[u // half, u % half], NT_DIMS, preferred_element_type=F32)
            part[stage, 0, u] = value[: 2 * rows].astype(BF16)
            part[stage, 1, u] = value[2 * rows :].astype(BF16)
        at = pl.ds(p * step, step)
        send(part.at[stage, 1 - c, at], core_in.at[stage, at], sem_c_out.at[stage], sem_c_in.at[stage, p], other)

    def pass_on(stage, p):
        at = pl.ds(p * step, step)
        wait_bytes(core_in.at[stage, at], sem_c_in.at[stage, p])
        when(stage > 0, lambda: wait_bytes(ring_in.at[stage, at], sem_r_in.at[stage, p]))
        for u in range(p * step, (p + 1) * step):
            value = part[stage, c, u].astype(F32) + core_in[stage, u].astype(F32) + ring_in[stage, u].astype(F32)
            ring_out[stage, u] = value.astype(BF16)
        if not isinstance(stage, int):
            send(ring_out.at[stage, at], ring_in.at[stage + 1, at], sem_r_out.at[stage], sem_r_in.at[stage + 1, p], onward)

    transform_s(0)
    for p in range(parts):
        multiply(0, p)

    def stage_step(stage, carry):
        when(stage == min(7, zs - 1), add_projection)
        transform_s(stage)
        for p in range(parts):
            multiply(stage, p)
            pass_on(stage - 1, p)
        return carry

    lax.fori_loop(1, zs, stage_step, 0)

    for n in range(pieces):
        for p in range(n * parts // pieces, (n + 1) * parts // pieces):
            pass_on(zs - 1, p)
        for xx in range(2):
            at = slice(xx * rows, (xx + 1) * rows)
            both = [
                (ring_out[zs - 1, n * half + f, at, :lane].astype(F32), ring_out[zs - 1, n * half + f, at, lane:].astype(F32))
                for f in range(half)
            ]
            values = backward([(both[0][0], None)] + both[1:] + [(both[0][1], None)])
            for k in range(total_k):
                p_out[n, xx, k // kpts, k % kpts] = (values[k] * (1.0 / total_k)).astype(BF16)
        pltpu.make_async_copy(p_out.at[n, xh, gb], p_in.at[n, gb, xh], sem_p.at[1, n]).start()

        def send_p(i, carry):
            peer, xx = (gb + groups // 2 + i // 2) % groups, (xh + i) % 2
            send(p_out.at[n, xx, peer], p_in.at[n, gb, xh], sem_p.at[0, n], sem_p.at[1, n], {"blk": peer, "tr": place(z, xx, c)})
            return carry

        lax.fori_loop(0, groups, send_p, 0)
        lax.fori_loop(groups + 1, 2 * groups, send_p, 0)

    exchange()

    own_t = count // (4 * zs)
    for n in range(pieces):
        cols = slice(n * lane, (n + 1) * lane)
        wait_bytes(p_in.at[n], sem_p.at[1, n])
        for k in range(kpts):
            for g in range(groups):
                value = p_in[n, g, 0, k].astype(F32) + p_in[n, g, 1, k].astype(F32)
                prhs[(k * groups + g) * rows : (k * groups + g + 1) * rows, cols] = value.astype(BF16)
        for m in range(zs // 2):
            at = slice(m * 8 * own_t, (m + 1) * 8 * own_t)
            value = eterm[at, cols] - jnp.dot(d2[at, :], prhs[:, cols], preferred_element_type=F32)
            for i in range(8):
                f_part[n, i % 2, m * 2 + i // 4, i // 2 % 2] = value[i * own_t : (i + 1) * own_t]
        send(f_part.at[n, 1 - c], f_core.at[n], sem_f.at[0, n], sem_f.at[1, n], other)
    for n in range(pieces):
        wait_bytes(f_core.at[n], sem_f.at[1, n])
        t_out[n] = (f_part[n, c] + f_core[n]).astype(BF16)
        pltpu.make_async_copy(t_out.at[n, z, xh], t_in.at[n, z, xh], sem_t.at[1, n]).start()

        def send_t(i, carry):
            zz, xx = (z + zs // 2 + i // 2) % zs, (xh + i) % 2
            send(t_out.at[n, zz, xx], t_in.at[n, z, xh], sem_t.at[0, n], sem_t.at[1, n], {"tr": place(zz, xx, c)})
            return carry

        lax.fori_loop(0, zs, send_t, 0)
        lax.fori_loop(zs + 1, 2 * zs, send_t, 0)
    square = lax.broadcasted_iota(jnp.int32, (own_t, own_t), 0) == lax.broadcasted_iota(jnp.int32, (own_t, own_t), 1)
    level = jnp.sum(jnp.where(square, jnp.broadcast_to(en[...], (own_t, own_t)), 0.0), axis=1, keepdims=True)
    mine = pl.ds(pl.multiple_of(me * own_t, own_t), own_t)
    for n in range(pieces):
        total = level * t[mine, n * lane : (n + 1) * lane].astype(F32)
        wait_bytes(t_in.at[n], sem_t.at[1, n])
        for zz in range(zs):
            for xx in range(2):
                total = total + t_in[n, zz, xx].astype(F32)
        out[:, n * lane : (n + 1) * lane] = total

    def sent_stage(stage, carry):
        wait_bytes(s_in.at[stage, pl.ds(0, groups - 1)], sem_s_out.at[stage])
        wait_bytes(core_in.at[stage], sem_c_out.at[stage])

        @pl.when(stage < zs - 1)
        def _():
            wait_bytes(ring_out.at[stage], sem_r_out.at[stage])

        return carry

    lax.fori_loop(0, zs, sent_stage, 0)
    wait_bytes(b_in.at[pl.ds(0, groups - 1)], sem_b_out)
    wait_bytes(proj_in.at[pl.ds(0, groups - 1)], sem_x.at[0])
    wait_bytes(scaled.at[:, pl.ds(0, (groups - 1) * share)], sem_x.at[2])
    for n in range(pieces):
        wait_bytes(p_in.at[n, pl.ds(0, groups - 1)], sem_p.at[0, n])
        wait_bytes(p_in.at[n, 0, 0], sem_p.at[0, n])
        wait_bytes(f_core.at[n], sem_f.at[0, n])
        wait_bytes(t_in.at[n, pl.ds(0, zs - 1)], sem_t.at[0, n])
        wait_bytes(t_in.at[n, 0, 0], sem_t.at[0, n])


def per_device(trial, energies, kpoint_of, exchange_dens, direct_dens, coulomb, screened):
    groups, members = lax.axis_size("blk"), lax.axis_size("tr")
    kpts, all_waves, waves = screened.shape
    count, vecs = trial.shape
    zs = members // 4
    rows = all_waves // groups // members
    half = groups * kpts // 2
    own_waves = exchange_dens.shape[1]
    share = own_waves // groups
    own_t = count // members
    parts, pieces = 8, 2
    lane = vecs // pieces
    units = pieces * half
    ys = groups // 2
    dma, vmem = pltpu.SemaphoreType.DMA, pltpu.VMEM
    scratch = [
        vmem((count, own_waves), BF16),
        vmem((count, waves), BF16),
        vmem((count, vecs), BF16),
        vmem((vecs, count), BF16),
        vmem((count, kpts * waves), BF16),
        vmem((zs, groups, 2, kpts, 2, rows, waves), BF16),
        vmem((pieces, kpts, lane, waves), BF16),
        vmem((groups, pieces, kpts, lane, waves), BF16),
        vmem((pieces, half, 2 * lane, 2 * waves), BF16),
        vmem((half, 4 * rows, 2 * waves), BF16),
        vmem((zs, 2, units, 2 * rows, 2 * lane), BF16),
        vmem((zs, units, 2 * rows, 2 * lane), BF16),
        vmem((zs, units, 2 * rows, 2 * lane), BF16),
        vmem((zs, units, 2 * rows, 2 * lane), BF16),
        vmem((ys, 2, vecs, share), F32),
        vmem((ys, 2, vecs, share), BF16),
        vmem((groups, vecs, share), BF16),
        vmem((vecs, own_waves), BF16),
        vmem((count, vecs), F32),
        vmem((pieces, 2, groups, kpts, rows, lane), BF16),
        vmem((pieces, groups, 2, kpts, rows, lane), BF16),
        vmem((kpts * groups * rows, vecs), BF16),
        vmem((pieces, 2, zs, 2, own_t, lane), F32),
        vmem((pieces, zs, 2, own_t, lane), F32),
        vmem((pieces, zs, 2, own_t, lane), BF16),
        vmem((pieces, zs, 2, own_t, lane), BF16),
        dma((3,)),
        dma((zs,)),
        dma((zs,)),
        dma,
        dma((ys + 1,)),
        dma((4,)),
        dma((zs,)),
        dma((zs, parts)),
        dma((zs,)),
        dma((zs, parts)),
        dma((2, pieces)),
        dma((2, pieces)),
        dma((2, pieces)),
    ]
    anywhere, in_vmem = pl.BlockSpec(memory_space=pl.ANY), pl.BlockSpec(memory_space=pltpu.VMEM)
    return pl.pallas_call(
        functools.partial(kernel, (groups, zs, kpts, rows, waves, vecs, parts, pieces)),
        out_shape=jax.ShapeDtypeStruct((own_t, vecs), F32),
        in_specs=[anywhere] * 4 + [in_vmem] * 3,
        out_specs=in_vmem,
        scratch_shapes=scratch,
        compiler_params=pltpu.CompilerParams(collective_id=0, has_side_effects=True, vmem_limit_bytes=63 * 1024 * 1024),
    )(
        screened.reshape(kpts, zs, 2, 2, groups, rows, waves),
        exchange_dens,
        direct_dens,
        trial,
        kpoint_of.reshape(1, count),
        coulomb.reshape(groups, share),
        energies.reshape(1, own_t),
    )


def solution(mesh):
    in_specs = (
        P("blk", None),
        P(("blk", "tr")),
        P("blk"),
        P("blk", "tr"),
        P("blk", "tr"),
        P("tr"),
        P("blk", None, "tr"),
    )
    out_specs = P(("blk", "tr"), None)
    return jax.shard_map(
        per_device, mesh=mesh, in_specs=in_specs, out_specs=out_specs, check_vma=False
    )
```

```python
import functools
import math

import jax
import jax.numpy as jnp
from jax import lax
from jax.experimental import pallas as pl
from jax.experimental.pallas import tpu as pltpu
from jax.sharding import PartitionSpec as P

F32, BF16 = jnp.float32, jnp.bfloat16
NT_DIMS = (((1,), (1,)), ((), ()))


def turn(value, angle):
    re, im = value
    c, s = math.cos(angle), math.sin(angle)
    if abs(s) < 1e-9:
        return value
    if abs(c) < 1e-9:
        return (None if im is None else -s * im), s * re
    if im is None:
        return c * re, s * re
    return c * re - s * im, s * re + c * im


def plus(a, b):
    return b if a is None else a if b is None else a + b


def minus(a, b):
    return a if b is None else -b if a is None else a - b


def forward(x):
    n = len(x)
    if n == 2:
        return [(x[0] + x[1], None), (x[0] - x[1], None)]
    even, odd = forward(x[0::2]), forward(x[1::2])
    out = [None] * (n // 2 + 1)
    for w in range(n // 4 + 1):
        e, o = even[w], turn(odd[w], -2 * math.pi * w / n)
        out[w] = plus(e[0], o[0]), plus(e[1], o[1])
        if w != n // 2 - w:
            re, im = minus(e[0], o[0]), minus(e[1], o[1])
            out[n // 2 - w] = re, None if im is None else -im
    return out


def backward(y):
    n = 2 * (len(y) - 1)
    if n == 2:
        return [y[0][0] + y[1][0], y[0][0] - y[1][0]]
    even, odd = [], []
    for w in range(n // 4 + 1):
        a, b = y[w], y[n // 2 - w]
        even.append((plus(a[0], b[0]), minus(a[1], b[1])))
        odd.append(turn((minus(a[0], b[0]), plus(a[1], b[1])), 2 * math.pi * w / n))
    for part in (even, odd):
        part[0], part[-1] = (part[0][0], None), (part[-1][0], None)
    out = [None] * n
    out[0::2], out[1::2] = backward(even), backward(odd)
    return out


def wait_bytes(ref, sem):
    pltpu.make_async_copy(ref, ref, sem).wait()


def send(src, dst, send_sem, recv_sem, device):
    pltpu.make_async_remote_copy(
        src_ref=src, dst_ref=dst, send_sem=send_sem, recv_sem=recv_sem,
        device_id=device, device_id_type=pl.DeviceIdType.MESH,
    ).start()


def when(condition, do):
    if isinstance(condition, bool):
        if condition:
            do()
    else:

        @pl.when(condition)
        def _():
            do()


def kernel(
    sizes, s_hbm, e_hbm, d_hbm, t_hbm, kp, coul, en, out,
    e, d, t, tt, d2, s_in, b_out, b_in, rhs, lhs, part, core_in, ring_out, ring_in,
    proj, proj_out, proj_in, scaled, eterm, p_out, p_in, prhs, f_part, f_core, t_out, t_in,
    sem_load, sem_s_out, sem_s_in, sem_b_out, sem_b_in, sem_x, sem_c_out, sem_c_in, sem_r_out, sem_r_in,
    sem_p, sem_f, sem_t,
):
    groups, zs, kpts, rows, waves, vecs, parts, pieces = sizes
    lane = vecs // pieces
    ys = groups // 2
    total_k = groups * kpts
    half = total_k // 2
    units = pieces * half
    step = units // parts
    gb = lax.axis_index("blk")
    me = lax.axis_index("tr")
    z, xh, c = me // 4, (me // 2) % 2, me % 2
    y, xl = gb // 2, gb % 2
    beside = y * 2 + 1 - xl

    def place(zz, xx, cc):
        return zz * 4 + xx * 2 + cc

    def along(j):
        return (gb + 2 * j) % groups

    other = {"tr": place(z, xh, 1 - c)}
    onward = {"tr": place((z + 1 - 2 * c + zs) % zs, xh, c)}

    loads = [pltpu.make_async_copy(a, b, sem_load.at[i]) for i, (a, b) in enumerate(((t_hbm, t), (d_hbm, d), (e_hbm, e)))]
    for load in loads:
        load.start()

    barrier = pltpu.get_barrier_semaphore()

    def greet(device):
        pl.semaphore_signal(barrier, inc=1, device_id=device, device_id_type=pl.DeviceIdType.MESH)

    greet(other)

    def greet_blk(i, carry):
        greet({"blk": (gb + i // 2) % groups, "tr": place(z, (xh + i) % 2, c)})
        return carry

    def greet_tr(i, carry):
        greet({"tr": place((z + i // 2) % zs, (xh + i) % 2, c)})
        return carry

    lax.fori_loop(1, 2 * groups, greet_blk, 0)
    lax.fori_loop(1, 2 * zs, greet_tr, 0)
    loads[0].wait()
    count = t.shape[0]
    tt[...] = t[...].T
    loads[1].wait()
    local = (kp[...] - gb * kpts).astype(F32)
    for k in range(kpts):
        mask = jnp.where(local == float(k), 1.0, 0.0).astype(BF16)
        own = jnp.dot(tt[...] * mask, d[...], preferred_element_type=F32)
        for n in range(pieces):
            b_out[n, k] = own[n * lane : (n + 1) * lane].astype(BF16)

    pl.semaphore_wait(barrier, 2 * groups + 2 * zs - 1)

    def send_s(stage, carry):
        for ab, zz in enumerate(((z - 1 - stage + 2 * zs) % zs, (z + 1 + stage) % zs)):
            pltpu.make_async_copy(s_hbm.at[:, zz, :, ab, gb], s_in.at[stage, gb, ab], sem_s_in.at[stage]).start()

        def to_peer(i, inner):
            peer = (gb + groups // 2 + i) % groups
            for ab, zz in enumerate(((z - 1 - stage + 2 * zs) % zs, (z + 1 + stage) % zs)):
                send(s_hbm.at[:, zz, :, ab, peer], s_in.at[stage, gb, ab], sem_s_out.at[stage], sem_s_in.at[stage], {"blk": peer})
            return inner

        lax.fori_loop(0, groups // 2, to_peer, 0)
        return lax.fori_loop(groups // 2 + 1, groups, to_peer, carry)

    rest = sem_b_in.at[ys]

    def send_block(src, slot, n, recv_sem, peer):
        send(src, b_in.at[slot, n], sem_b_out, recv_sem, {"blk": peer})

    send_block(b_out.at[0], gb, 0, sem_b_in.at[0], beside)
    for j in range(1, ys):
        send_block(b_out.at[1], gb, 1, sem_b_in.at[ys - j], along(j))
    send_block(b_out.at[1], gb, 1, rest, beside)
    for j in range(1, ys):
        send_block(b_out.at[0], gb, 0, rest, along(j))
    pltpu.make_async_copy(b_out, b_in.at[gb], rest).start()
    send_s(0, 0)

    loads[2].wait()
    own_waves = e.shape[1]
    share = own_waves // groups
    for i in range(ys):
        value = jnp.dot(tt[...], e[:, 2 * i * share : 2 * (i + 1) * share], preferred_element_type=F32)
        for j in range(2):
            proj[i, j] = value[:, j * share : (j + 1) * share]
            proj_out[i, j] = value[:, j * share : (j + 1) * share].astype(BF16)

    wait_bytes(b_in.at[0, 0], sem_b_in.at[0])
    for j in range(1, ys):
        send_block(b_in.at[beside, 0], beside, 0, rest, along(j))
    for j in range(1, ys):
        wait_bytes(b_in.at[0, 1], sem_b_in.at[j])
        send_block(b_in.at[along(j), 1], along(j), 1, rest, beside)

    def cut(index):
        return pl.ds(pl.multiple_of(index * share, share), share)

    far_first = [i % groups for i in range(groups // 2, groups // 2 + groups) if i != groups]

    def send_projection():
        for i in far_first:
            peer = (gb + i) % groups
            send(proj_out.at[peer // 2, peer % 2], proj_in.at[gb], sem_x.at[0], sem_x.at[1], {"blk": peer})

    def add_projection():
        wait_bytes(proj_in.at[pl.ds(0, groups - 1)], sem_x.at[1])
        total = proj[y, xl]
        for i in range(1, groups):
            total = total + proj_in[(gb + i) % groups].astype(F32)
        scaled[:, cut(gb)] = (coul[pl.ds(gb, 1), :] * total).astype(BF16)
        for i in far_first:
            send(scaled.at[:, cut(gb)], scaled.at[:, cut(gb)], sem_x.at[2], sem_x.at[3], {"blk": (gb + i) % groups})

    lax.fori_loop(min(1, zs), min(8, zs), send_s, 0)
    send_projection()

    ring_in[0] = jnp.zeros(ring_in.shape[1:], BF16)
    unit = min(128, count)
    eye = lax.broadcasted_iota(jnp.int32, (unit, unit), 0) == lax.broadcasted_iota(jnp.int32, (unit, unit), 1)
    for i in range(count // unit):
        at = slice(i * unit, (i + 1) * unit)
        column = jnp.sum(jnp.where(eye, jnp.broadcast_to(local[:, at], (unit, unit)), 0.0), axis=1, keepdims=True)
        dens = d[at, :].astype(F32)
        for k in range(kpts):
            d2[at, k * waves : (k + 1) * waves] = (dens * jnp.where(column == float(k), 1.0, 0.0)).astype(BF16)

    wait_bytes(b_in.at[pl.ds(0, 3 * ys // 2)], rest)
    tile = min(16, lane)

    def transform_b(i, carry):
        n, row = i // (lane // tile), i % (lane // tile) * tile
        at = pl.ds(pl.multiple_of(row, tile), tile)
        low = pl.ds(pl.multiple_of(lane + row, tile), tile)
        freq = forward([b_in[q // kpts, n, q % kpts, at, :].astype(F32) for q in range(total_k)])
        zero = jnp.zeros((tile, waves), BF16)
        for f in range(half):
            re, im = (freq[0][0], freq[half][0]) if f == 0 else freq[f]
            re, im = re.astype(BF16), im.astype(BF16)
            rhs[n, f, at, 0:waves] = re
            rhs[n, f, at, waves:] = zero if f == 0 else -im
            rhs[n, f, low, 0:waves] = zero if f == 0 else im
            rhs[n, f, low, waves:] = im if f == 0 else re
        return carry

    lax.fori_loop(0, vecs // tile, transform_b, 0)

    def exchange():
        wait_bytes(scaled.at[:, pl.ds(0, (groups - 1) * share)], sem_x.at[3])
        chunk_t = min(256, count)

        def do(i, carry):
            at = pl.ds(pl.multiple_of(i * chunk_t, chunk_t), chunk_t)
            eterm[at, :] = 2.0 * lax.dot_general(e[at, :], scaled[...], NT_DIMS, preferred_element_type=F32)
            return carry

        lax.fori_loop(0, count // chunk_t, do, 0)

    def transform_s(stage):
        wait_bytes(s_in.at[stage], sem_s_in.at[stage])
        for ab in range(2):
            for xx in range(2):
                freq = forward([s_in[stage, q // kpts, ab, q % kpts, xx].astype(F32) for q in range(total_k)])
                at = slice((ab * 2 + xx) * rows, (ab * 2 + xx + 1) * rows)
                for f in range(half):
                    re, im = (freq[0][0], freq[half][0]) if f == 0 else freq[f]
                    lhs[f, at, 0:waves] = re.astype(BF16)
                    lhs[f, at, waves:] = im.astype(BF16)

    def multiply(stage, p):
        for u in range(p * step, (p + 1) * step):
            value = lax.dot_general(lhs[u % half], rhs[u // half, u % half], NT_DIMS, preferred_element_type=F32)
            part[stage, 0, u] = value[: 2 * rows].astype(BF16)
            part[stage, 1, u] = value[2 * rows :].astype(BF16)
        at = pl.ds(p * step, step)
        send(part.at[stage, 1 - c, at], core_in.at[stage, at], sem_c_out.at[stage], sem_c_in.at[stage, p], other)

    def pass_on(stage, p):
        at = pl.ds(p * step, step)
        wait_bytes(core_in.at[stage, at], sem_c_in.at[stage, p])
        when(stage > 0, lambda: wait_bytes(ring_in.at[stage, at], sem_r_in.at[stage, p]))
        for u in range(p * step, (p + 1) * step):
            value = part[stage, c, u].astype(F32) + core_in[stage, u].astype(F32) + ring_in[stage, u].astype(F32)
            ring_out[stage, u] = value.astype(BF16)
        if not isinstance(stage, int):
            send(ring_out.at[stage, at], ring_in.at[stage + 1, at], sem_r_out.at[stage], sem_r_in.at[stage + 1, p], onward)

    transform_s(0)
    for p in range(parts):
        multiply(0, p)

    def stage_step(stage, carry):
        when(stage == min(7, zs - 1), add_projection)
        transform_s(stage)
        for p in range(parts):
            multiply(stage, p)
            pass_on(stage - 1, p)
        return carry

    lax.fori_loop(1, zs, stage_step, 0)

    for n in range(pieces):
        for p in range(n * parts // pieces, (n + 1) * parts // pieces):
            pass_on(zs - 1, p)
        for xx in range(2):
            at = slice(xx * rows, (xx + 1) * rows)
            both = [
                (ring_out[zs - 1, n * half + f, at, :lane].astype(F32), ring_out[zs - 1, n * half + f, at, lane:].astype(F32))
                for f in range(half)
            ]
            values = backward([(both[0][0], None)] + both[1:] + [(both[0][1], None)])
            for k in range(total_k):
                p_out[n, xx, k // kpts, k % kpts] = (values[k] * (1.0 / total_k)).astype(BF16)
        pltpu.make_async_copy(p_out.at[n, xh, gb], p_in.at[n, gb, xh], sem_p.at[1, n]).start()

        def send_p(i, carry):
            peer, xx = (gb + groups // 2 + i // 2) % groups, (xh + i) % 2
            send(p_out.at[n, xx, peer], p_in.at[n, gb, xh], sem_p.at[0, n], sem_p.at[1, n], {"blk": peer, "tr": place(z, xx, c)})
            return carry

        lax.fori_loop(0, groups, send_p, 0)
        lax.fori_loop(groups + 1, 2 * groups, send_p, 0)

    exchange()

    own_t = count // (4 * zs)
    for n in range(pieces):
        cols = slice(n * lane, (n + 1) * lane)
        wait_bytes(p_in.at[n], sem_p.at[1, n])
        for k in range(kpts):
            for g in range(groups):
                value = p_in[n, g, 0, k].astype(F32) + p_in[n, g, 1, k].astype(F32)
                prhs[(k * groups + g) * rows : (k * groups + g + 1) * rows, cols] = value.astype(BF16)
        for m in range(zs // 2):
            at = slice(m * 8 * own_t, (m + 1) * 8 * own_t)
            value = eterm[at, cols] - jnp.dot(d2[at, :], prhs[:, cols], preferred_element_type=F32)
            for i in range(8):
                f_part[n, i % 2, m * 2 + i // 4, i // 2 % 2] = value[i * own_t : (i + 1) * own_t]
        send(f_part.at[n, 1 - c], f_core.at[n], sem_f.at[0, n], sem_f.at[1, n], other)
    for n in range(pieces):
        wait_bytes(f_core.at[n], sem_f.at[1, n])
        t_out[n] = (f_part[n, c] + f_core[n]).astype(BF16)
        pltpu.make_async_copy(t_out.at[n, z, xh], t_in.at[n, z, xh], sem_t.at[1, n]).start()

        def send_t(i, carry):
            zz, xx = (z + zs // 2 + i // 2) % zs, (xh + i) % 2
            send(t_out.at[n, zz, xx], t_in.at[n, z, xh], sem_t.at[0, n], sem_t.at[1, n], {"tr": place(zz, xx, c)})
            return carry

        lax.fori_loop(0, zs, send_t, 0)
        lax.fori_loop(zs + 1, 2 * zs, send_t, 0)
    square = lax.broadcasted_iota(jnp.int32, (own_t, own_t), 0) == lax.broadcasted_iota(jnp.int32, (own_t, own_t), 1)
    level = jnp.sum(jnp.where(square, jnp.broadcast_to(en[...], (own_t, own_t)), 0.0), axis=1, keepdims=True)
    mine = pl.ds(pl.multiple_of(me * own_t, own_t), own_t)
    for n in range(pieces):
        total = level * t[mine, n * lane : (n + 1) * lane].astype(F32)
        wait_bytes(t_in.at[n], sem_t.at[1, n])
        for zz in range(zs):
            for xx in range(2):
                total = total + t_in[n, zz, xx].astype(F32)
        out[:, n * lane : (n + 1) * lane] = total

    def sent_stage(stage, carry):
        wait_bytes(s_in.at[stage, pl.ds(0, groups - 1)], sem_s_out.at[stage])
        wait_bytes(core_in.at[stage], sem_c_out.at[stage])

        @pl.when(stage < zs - 1)
        def _():
            wait_bytes(ring_out.at[stage], sem_r_out.at[stage])

        return carry

    lax.fori_loop(0, zs, sent_stage, 0)
    wait_bytes(b_in.at[pl.ds(0, groups - 1)], sem_b_out)
    wait_bytes(proj_in.at[pl.ds(0, groups - 1)], sem_x.at[0])
    wait_bytes(scaled.at[:, pl.ds(0, (groups - 1) * share)], sem_x.at[2])
    for n in range(pieces):
        wait_bytes(p_in.at[n, pl.ds(0, groups - 1)], sem_p.at[0, n])
        wait_bytes(p_in.at[n, 0, 0], sem_p.at[0, n])
        wait_bytes(f_core.at[n], sem_f.at[0, n])
        wait_bytes(t_in.at[n, pl.ds(0, zs - 1)], sem_t.at[0, n])
        wait_bytes(t_in.at[n, 0, 0], sem_t.at[0, n])


def per_device(trial, energies, kpoint_of, exchange_dens, direct_dens, coulomb, screened):
    groups, members = lax.axis_size("blk"), lax.axis_size("tr")
    kpts, all_waves, waves = screened.shape
    count, vecs = trial.shape
    zs = members // 4
    rows = all_waves // groups // members
    half = groups * kpts // 2
    own_waves = exchange_dens.shape[1]
    share = own_waves // groups
    own_t = count // members
    parts, pieces = 8, 2
    lane = vecs // pieces
    units = pieces * half
    ys = groups // 2
    dma, vmem = pltpu.SemaphoreType.DMA, pltpu.VMEM
    scratch = [
        vmem((count, own_waves), BF16),
        vmem((count, waves), BF16),
        vmem((count, vecs), BF16),
        vmem((vecs, count), BF16),
        vmem((count, kpts * waves), BF16),
        vmem((zs, groups, 2, kpts, 2, rows, waves), BF16),
        vmem((pieces, kpts, lane, waves), BF16),
        vmem((groups, pieces, kpts, lane, waves), BF16),
        vmem((pieces, half, 2 * lane, 2 * waves), BF16),
        vmem((half, 4 * rows, 2 * waves), BF16),
        vmem((zs, 2, units, 2 * rows, 2 * lane), BF16),
        vmem((zs, units, 2 * rows, 2 * lane), BF16),
        vmem((zs, units, 2 * rows, 2 * lane), BF16),
        vmem((zs, units, 2 * rows, 2 * lane), BF16),
        vmem((ys, 2, vecs, share), F32),
        vmem((ys, 2, vecs, share), BF16),
        vmem((groups, vecs, share), BF16),
        vmem((vecs, own_waves), BF16),
        vmem((count, vecs), F32),
        vmem((pieces, 2, groups, kpts, rows, lane), BF16),
        vmem((pieces, groups, 2, kpts, rows, lane), BF16),
        vmem((kpts * groups * rows, vecs), BF16),
        vmem((pieces, 2, zs, 2, own_t, lane), F32),
        vmem((pieces, zs, 2, own_t, lane), F32),
        vmem((pieces, zs, 2, own_t, lane), BF16),
        vmem((pieces, zs, 2, own_t, lane), BF16),
        dma((3,)),
        dma((zs,)),
        dma((zs,)),
        dma,
        dma((ys + 1,)),
        dma((4,)),
        dma((zs,)),
        dma((zs, parts)),
        dma((zs,)),
        dma((zs, parts)),
        dma((2, pieces)),
        dma((2, pieces)),
        dma((2, pieces)),
    ]
    anywhere, in_vmem = pl.BlockSpec(memory_space=pl.ANY), pl.BlockSpec(memory_space=pltpu.VMEM)
    return pl.pallas_call(
        functools.partial(kernel, (groups, zs, kpts, rows, waves, vecs, parts, pieces)),
        out_shape=jax.ShapeDtypeStruct((own_t, vecs), F32),
        in_specs=[anywhere] * 4 + [in_vmem] * 3,
        out_specs=in_vmem,
        scratch_shapes=scratch,
        compiler_params=pltpu.CompilerParams(collective_id=0, has_side_effects=True, vmem_limit_bytes=63 * 1024 * 1024),
    )(
        screened.reshape(kpts, zs, 2, 2, groups, rows, waves),
        exchange_dens,
        direct_dens,
        trial,
        kpoint_of.reshape(1, count),
        coulomb.reshape(groups, share),
        energies.reshape(1, own_t),
    )


def solution(mesh):
    in_specs = (
        P("blk", None),
        P(("blk", "tr")),
        P("blk"),
        P("blk", "tr"),
        P("blk", "tr"),
        P("tr"),
        P("blk", None, "tr"),
    )
    out_specs = P(("blk", "tr"), None)
    return jax.shard_map(
        per_device, mesh=mesh, in_specs=in_specs, out_specs=out_specs, check_vma=False
    )
```
